32 devices in a mesh: group: 4 (over y, x), member: 8 (over z, core).
Axes of the slice: x: 2, y: 2, z: 4, core: 2. Of those that a mesh axis runs over, the one named last changes fastest.
Arguments:
- embeddings: bfloat16 [1024, 39, 128], P(('group', 'member')), may hold values from -6 to 6
- cot_first: bfloat16 [1024, 100], P(('group', 'member')), may hold values from -6 to 6
- cot_second: bfloat16 [1024, 100], P(('group', 'member')), may hold values from -6 to 6
- cot_third: bfloat16 [1024, 100], P(('group', 'member')), may hold values from -6 to 6
- w_first: bfloat16 [100, 39, 39], replicated, may hold values from -0.15625 to 0.15625
- w_second: bfloat16 [100, 100, 39], replicated, may hold values from -0.09375 to 0.09375
- w_third: bfloat16 [100, 100, 39], replicated, may hold values from -0.09375 to 0.09375
- unique_ids: int32 [32, 96], P(('group', 'member')), may hold values from 0 to 131071, as said below
- inverse: int32 [1024, 39], P(('group', 'member')), may hold values from 0 to 95, as said below
- table: float32 [131072, 128], P(('group', 'member')), may hold values from -6 to 6
- accum: float32 [131072], P(('group', 'member')), may hold values from 1 to 300
- next_ids: int32 [32, 192], P(('group', 'member')), may hold values from 0 to 131071, as said below
Outputs:
- new_table: float32 [131072, 128], P(('group', 'member'))
- new_accum: float32 [131072], P(('group', 'member'))
- returned: float32 [32, 192, 128], P(('group', 'member'))
The draws below stay inside these ranges and needn't reach their ends.
Inputs may be any that keep to these rules, and one draw needn't show every extreme that they name: `unique_ids`: row s lists 96 distinct table rows looked up by the samples of device s along group+member, ordered so that the owner r // 4096 never falls; at most 4 rows of one list have the same owner. `inverse`: lookup (n, f) names a position in row n // 32 of unique_ids; every position of a row is named by some lookup. `next_ids`: row s lists 192 distinct table rows read by device s, ordered so that the owner r // 4096 never falls; at most 8 rows of one list have the same owner.
All inputs are finite; a program needn't handle non-finite values.
Results may differ from the reference program's by a relative error of at most 0.0007.
Values sent between devices are 32-bit elements; how exact they have to be, the bound alone decides.
No kernel may reach another device: no remote copies, remote signals or barrier semaphores. Data moves between devices by JAX's collectives and lax.ppermute only.
A program may use at most 64 MiB of HBM per device.

```python
import math
import jax
import jax.numpy as jnp
from jax import lax

FIELDS = 39
EMBED = 128
MAPS = 100
B_DEV = 32
ROWS_DEV = 4096
CAP = 4
RCAP = 8
SAMPLES = 1024
TABLE_ROWS = 131072
UNIQ = 96
NEXTQ = 192
N_GROUP = 4
N_MEMBER = 8


def bucketed_rows(key, capacity, length):
    devices = N_GROUP * N_MEMBER
    pair_count = devices * capacity
    hot_key, perm_key = jax.random.split(key)
    hottest = jax.random.randint(hot_key, (), 0, devices)

    def one_list(list_key):
        ranking_key, anchor_key = jax.random.split(list_key)
        ranking = jax.random.permutation(ranking_key, pair_count).astype(jnp.int32)
        indices = jnp.arange(pair_count, dtype=jnp.int32)
        owner_of = indices // capacity
        scores = jnp.where(owner_of == hottest, indices % capacity - pair_count, ranking)
        chosen = jnp.sort(jnp.argsort(scores)[:length].astype(jnp.int32) // capacity)
        leading = jnp.searchsorted(chosen, chosen, side='left').astype(jnp.int32)
        within = jnp.arange(length, dtype=jnp.int32) - leading
        anchor = jax.random.randint(anchor_key, (devices,), 0, ROWS_DEV)
        inside = (anchor[chosen] + within * (ROWS_DEV // capacity)) % ROWS_DEV
        return chosen * ROWS_DEV + inside
    return jax.vmap(one_list)(jax.random.split(perm_key, devices))


def draw_unique_ids(key, part):
    return bucketed_rows(jax.random.fold_in(key, 17), CAP, UNIQ)


def draw_next_ids(key, part):
    return bucketed_rows(jax.random.fold_in(key, 29), RCAP, NEXTQ)


def draw_inverse(key, part):
    devices = N_GROUP * N_MEMBER
    lookups = B_DEV * FIELDS

    def one_list(list_key):
        repeat_key, shuffle_key = jax.random.split(list_key)
        repeats = jax.random.randint(repeat_key, (lookups - UNIQ,), 0, UNIQ)
        complete = jnp.concatenate([jnp.arange(UNIQ, dtype=jnp.int32), repeats.astype(jnp.int32)])
        return jax.random.permutation(shuffle_key, complete)
    lists = jax.vmap(one_list)(jax.random.split(jax.random.fold_in(key, 41), devices))
    return lists.reshape(devices * B_DEV, FIELDS)


def block_scale(rng, extent, cuts, low, top_value):
    gain = 1.0
    for dim, blocks in cuts:
        draws = jax.random.uniform(jax.random.fold_in(jax.random.fold_in(rng, 6), dim), (blocks,), jnp.float32, low / len(cuts), top_value / len(cuts))
        gain = gain * jnp.repeat(jnp.exp(draws), extent[dim] // blocks).reshape((-1,) + (1,) * (len(extent) - 1 - dim))
    return gain


def bell_draw(key, extent, spread, reach, cuts=(), kind=jnp.bfloat16):
    drawn = spread * jax.random.normal(key, extent, jnp.float32)
    if cuts:
        drawn = drawn * block_scale(key, extent, cuts, -0.22, 0.18)
    return jnp.clip(drawn, -reach, reach).astype(kind)


def setup_inputs(seed: int = 0) -> dict:
    keys = jax.random.split(jax.random.key(seed), 13)
    embeddings = bell_draw(keys[0], (SAMPLES, FIELDS, EMBED), 1.0, 6.0, ((0, 32),))
    cot_first = bell_draw(keys[1], (SAMPLES, MAPS), 1.0, 6.0, ((0, 32),))
    cot_second = bell_draw(keys[2], (SAMPLES, MAPS), 1.0, 6.0, ((0, 32),))
    cot_third = bell_draw(keys[3], (SAMPLES, MAPS), 1.0, 6.0, ((0, 32),))
    w_first = bell_draw(keys[4], (MAPS, FIELDS, FIELDS), (FIELDS * FIELDS) ** -0.5, 0.15625)
    w_second = bell_draw(keys[5], (MAPS, MAPS, FIELDS), (MAPS * FIELDS) ** -0.5, 0.09375)
    w_third = bell_draw(keys[6], (MAPS, MAPS, FIELDS), (MAPS * FIELDS) ** -0.5, 0.09375)
    unique_ids = draw_unique_ids(jax.random.fold_in(keys[12], 71), 0)
    inverse = draw_inverse(jax.random.fold_in(keys[12], 71), 0)
    table = bell_draw(keys[9], (TABLE_ROWS, EMBED), 1.0, 6.0, ((0, 32),), jnp.float32)
    accum = jnp.clip(jnp.exp(math.log(300.0) - 5.7037825 * jax.random.uniform(keys[10], (TABLE_ROWS,), jnp.float32) ** block_scale(keys[10], (TABLE_ROWS,), ((0, 32),), -0.2, 0.2)), 1.0, 300.0)
    next_ids = draw_next_ids(jax.random.fold_in(keys[12], 71), 0)
    return dict(embeddings=embeddings, cot_first=cot_first, cot_second=cot_second, cot_third=cot_third, w_first=w_first, w_second=w_second, w_third=w_third, unique_ids=unique_ids, inverse=inverse, table=table, accum=accum, next_ids=next_ids)


RATE = 0.5
EPS = 1e-08

def cin_block(inputs, first_cot, second_cot, third_cot, first_w, second_w, third_w):
    exact = lax.Precision.HIGHEST
    widened = inputs.astype(jnp.float32)
    pairs_one = (widened[:, :, None] * widened[:, None]).astype(jnp.bfloat16)
    layer_one = jnp.einsum('hij,nijd->nhd', first_w.astype(jnp.float32), pairs_one.astype(jnp.float32)).astype(jnp.bfloat16)
    one_wide = layer_one.astype(jnp.float32)
    pairs_two = (one_wide[:, :, None] * widened[:, None]).astype(jnp.bfloat16)
    layer_two = jnp.einsum('hij,nijd->nhd', second_w.astype(jnp.float32), pairs_two.astype(jnp.float32)).astype(jnp.bfloat16)
    two_wide = layer_two.astype(jnp.float32)
    top_map = jnp.einsum('hij,nh->nij', third_w.astype(jnp.float32), third_cot.astype(jnp.float32))
    grad_two = jnp.einsum('nij,njd->nid', top_map, widened, precision=exact)
    grad_base = jnp.einsum('nij,nid->njd', top_map, two_wide, precision=exact)
    upper = (second_cot.astype(jnp.float32)[:, :, None] + grad_two).astype(jnp.bfloat16)
    middle = jnp.einsum('hij,nhd->nijd', second_w.astype(jnp.float32), upper.astype(jnp.float32))
    grad_one = lax.optimization_barrier(jnp.sum(middle * widened[:, None], axis=2))
    grad_base = grad_base + lax.optimization_barrier(jnp.sum(middle * one_wide[:, :, None], axis=1))
    lower = (first_cot.astype(jnp.float32)[:, :, None] + grad_one).astype(jnp.bfloat16)
    bottom = jnp.einsum('hij,nhd->nijd', first_w.astype(jnp.float32), lower.astype(jnp.float32))
    grad_base = grad_base + lax.optimization_barrier(jnp.sum(bottom * widened[:, None], axis=2)) + lax.optimization_barrier(jnp.sum(bottom * widened[:, :, None], axis=1))
    return grad_base

def reference(embeddings, cot_first, cot_second, cot_third, w_first, w_second, w_third, unique_ids, inverse, table, accum, next_ids):
    devices = N_GROUP * N_MEMBER

    def one_device(pieces):
        return cin_block(pieces[0], pieces[1], pieces[2], pieces[3], w_first, w_second, w_third)
    pieces = (embeddings.reshape(devices, B_DEV, FIELDS, EMBED), cot_first.reshape(devices, B_DEV, MAPS), cot_second.reshape(devices, B_DEV, MAPS), cot_third.reshape(devices, B_DEV, MAPS))
    grads = lax.map(one_device, pieces)
    row_ids = jnp.take_along_axis(unique_ids, inverse.reshape(devices, B_DEV * FIELDS), axis=1)
    table_grad = jax.ops.segment_sum(grads.reshape(-1, EMBED), row_ids.reshape(-1), num_segments=TABLE_ROWS)
    new_accum = accum + lax.optimization_barrier(jnp.mean(table_grad * table_grad, axis=1))
    new_table = table - RATE * table_grad / (jnp.sqrt(new_accum) + EPS)[:, None]
    returned = jnp.take(new_table, next_ids, axis=0)
    return (new_table, new_accum, returned)
```

```python
import functools

import jax
import jax.numpy as jnp
from jax import lax
from jax.experimental import pallas as pl
from jax.experimental.pallas import tpu as pltpu
from jax.sharding import PartitionSpec as P

CAP = 4
RCAP = 8

RATE = 0.5
EPS = 1e-08

LANES = 128
SUB = 8
PACK = 16
SLOT = 8
BLOCK = 4

f32 = jnp.float32
bf16 = jnp.bfloat16


def up(value, unit):
    return -(-value // unit) * unit


def split(value):
    high = value.astype(bf16)
    return high, (value - high.astype(f32)).astype(bf16)


def mm(a, b):
    return jnp.dot(a, b, preferred_element_type=f32)


def mm_t(a, b):
    return lax.dot_general(a, b, (((0,), (0,)), ((), ())), preferred_element_type=f32)


def grad_kernel(
    fields,
    rows_dev,
    emb,
    c1,
    c2,
    c3,
    w1,
    w2,
    w3,
    uid,
    nid,
    inv,
    payload,
    xs,
    top,
    c1s,
    c3s,
    w1s,
    w1t,
    w2s,
    w2t,
    xf,
    xp,
    p1,
    p2,
    y1s,
    y2s,
    us,
    ls,
    acc,
    part,
    grad,
    merged,
):
    step = pl.program_id(0)
    samples = inv.shape[0]
    maps = c1.shape[1]
    fp = xf.shape[0]
    hp = acc.shape[0]
    hb = hp // SUB
    fb = fp // SUB
    pairs = fp // 2
    width = xf.shape[1]

    def offsets():
        place = 0
        for m in range(pairs):
            ib = (2 * m) // SUB
            for jb in range(ib, fb):
                yield m, ib, jb, place
                place += PACK

    @pl.when(step == 0)
    def _():
        xs[pl.ds(0, fields * samples), :] = (
            emb[...].astype(f32).reshape(fields * samples, LANES)
        )
        xs[pl.ds(fields * samples, samples), :] = jnp.zeros((samples, LANES), f32)
        c1s[...] = jnp.zeros_like(c1s)
        c1s[:, 0:maps] = c1[...]
        c3s[...] = jnp.zeros_like(c3s)
        c3s[:, 0:maps] = c3[...]
        for j in range(fields):
            top[pl.ds(j * samples, samples), :] = mm(c3s[...], w3[j])
        top[pl.ds(fields * samples, samples), :] = jnp.zeros((samples, LANES), f32)
        top[pl.ds(fields * samples, samples), 0:maps] = c2[...].astype(f32)
        for m in range(pairs):
            two = [
                w2[2 * m + s].astype(f32).T[0:hp].reshape(hb, SUB, LANES) for s in range(2)
            ]
            w2s[pl.ds(m * 2 * hp, 2 * hp), :] = (
                jnp.stack(two, axis=1).reshape(2 * hp, LANES).astype(bf16)
            )
        w2s[pl.ds(pairs * 2 * hp, w2s.shape[0] - pairs * 2 * hp), :] = jnp.zeros(
            (w2s.shape[0] - pairs * 2 * hp, LANES), bf16
        )
        for c in range(w2s.shape[0] // LANES):
            w2t[:, c * LANES : (c + 1) * LANES] = (
                w2s[c * LANES : (c + 1) * LANES, :].astype(f32).T[0:hp].astype(bf16)
            )
        w1s[...] = jnp.zeros_like(w1s)
        for m, ib, jb, place in offsets():
            two = [
                w1[2 * m + s, SUB * jb : SUB * (jb + 1), :].astype(f32) for s in range(2)
            ]
            w1s[pl.ds(place, PACK), :] = jnp.concatenate(two, axis=0).astype(bf16)
        for c in range(w1s.shape[0] // LANES):
            w1t[:, c * LANES : (c + 1) * LANES] = (
                w1s[c * LANES : (c + 1) * LANES, :].astype(f32).T[0:hp].astype(bf16)
            )
        us[...] = jnp.zeros_like(us)
        ls[...] = jnp.zeros_like(ls)
        y2s[...] = jnp.zeros_like(y2s)
        merged[...] = jnp.zeros_like(merged)

    first = step * BLOCK
    for k in range(BLOCK):
        xf[:, k * LANES : (k + 1) * LANES] = xs[pl.ds(first + k, fp, stride=samples), :]
    for m in range(pairs):
        xp[m] = jnp.concatenate(
            [jnp.broadcast_to(xf[2 * m + s : 2 * m + s + 1, :], (SUB, width)) for s in range(2)],
            axis=0,
        ).astype(bf16)
    twice = []
    for b in range(fb):
        block = xf[SUB * b : SUB * (b + 1), :]
        twice.append(jnp.concatenate([block, block], axis=0).astype(bf16))
    half = [t * jnp.asarray(0.5, bf16) for t in twice]
    for m, ib, jb, place in offsets():
        p1[pl.ds(place, PACK), :] = xp[m] * (half[jb] if jb == ib else twice[jb])
    layer_one = mm(w1t[:, 0 : p1.shape[0]], p1[...]).astype(bf16).astype(f32)
    y1s[...] = layer_one
    for b in range(hb):
        block = y1s[SUB * b : SUB * (b + 1), :]
        double = jnp.concatenate([block, block], axis=0).astype(bf16)
        for m in range(pairs):
            p2[pl.ds(m * 2 * hp + b * PACK, PACK), :] = xp[m] * double
    y2s[0:hp, :] = mm(w2t[:, 0 : p2.shape[0]], p2[...]).astype(bf16)

    last_row = lax.broadcasted_iota(jnp.int32, (fp, LANES), 0) == fields
    tops = []
    for k in range(BLOCK):
        here = slice(k * LANES, (k + 1) * LANES)
        high, low = split(top[pl.ds(first + k, fp, stride=samples), :])
        tops.append((high, low))
        own = jnp.where(last_row, 1.0, xf[:, here]).astype(bf16)
        us[:, here] = mm_t(
            jnp.concatenate([high, low], axis=0), jnp.concatenate([own, own], axis=0)
        ).astype(bf16)

    pick = (
        lax.broadcasted_iota(jnp.int32, (samples, width), 0)
        == first + lax.broadcasted_iota(jnp.int32, (samples, width), 1) // LANES
    )
    acc[...] = mm_t(c1s[...], pick.astype(bf16))[0:hp]
    group = 2
    for m0 in range(0, pairs, group):
        z = mm(w2s[m0 * 2 * hp : (m0 + group) * 2 * hp, :], us[...])
        z = z.reshape(group, hb, 2, SUB, width)
        total = None
        for g in range(group):
            for s in range(2):
                j = 2 * (m0 + g) + s
                zj = z[g, :, s].reshape(hp, width)
                if j < fields:
                    term = zj * xf[j : j + 1, :]
                    total = term if total is None else total + term
                folded = (zj * y1s[...]).reshape(hb, SUB, width).sum(0)
                for k in range(BLOCK):
                    part[pl.ds((k * fp + j) * SUB, SUB), :] = folded[
                        :, k * LANES : (k + 1) * LANES
                    ]
        acc[...] += total
    ls[0:hp, :] = acc[...].astype(bf16)

    grad[...] = jnp.zeros_like(grad)
    z = mm(w1s[0 : p1.shape[0], :], ls[...])
    for m in range(pairs):
        ib = (2 * m) // SUB
        place = [q for q in offsets() if q[0] == m]
        for s in range(2):
            i = 2 * m + s
            across = None
            for _, _, jb, at in place:
                zj = z[at + SUB * s : at + SUB * (s + 1)]
                grad[SUB * jb : SUB * (jb + 1), :] += zj * xf[i : i + 1, :]
                if jb > ib:
                    term = zj * xf[SUB * jb : SUB * (jb + 1), :]
                    across = term if across is None else across + term
            if across is not None:
                for k in range(BLOCK):
                    part[pl.ds((k * fp + i) * SUB, SUB), :] += across[
                        :, k * LANES : (k + 1) * LANES
                    ]

    positions = merged.shape[0]
    for k in range(BLOCK):
        here = slice(k * LANES, (k + 1) * LANES)
        mine = grad[:, here]
        for s in range(SUB):
            mine = mine + part[pl.ds(k * fp * SUB + s, fp, stride=SUB), :]
        high, low = tops[k]
        y2 = y2s[:, here]
        mine = mine + mm(jnp.concatenate([high, low], axis=1), jnp.concatenate([y2, y2], axis=0))
        named = inv[pl.ds(first + k, 1), :]
        chosen = (
            lax.broadcasted_iota(jnp.int32, (positions, fields), 0)
            == jnp.broadcast_to(named, (positions, fields))
        ).astype(bf16)
        high, low = split(mine[0:fields])
        merged[...] += mm(chosen, high) + mm(chosen, low)

    @pl.when(step == pl.num_programs(0) - 1)
    def _():
        owners = payload.shape[0] // SLOT
        rows = owners * SLOT

        listed = uid[...]
        wanted = nid[...]
        row = lax.broadcasted_iota(jnp.int32, (rows, 1), 0)
        owner = row // SLOT
        slot = row % SLOT
        bottom = owner * rows_dev
        start = jnp.sum((listed < bottom).astype(f32), axis=1, keepdims=True).astype(jnp.int32)
        at = lax.broadcasted_iota(jnp.int32, (rows, positions), 1)
        inside = (listed >= bottom) & (listed < bottom + rows_dev)
        chosen = ((at == start + slot) & inside & (slot < CAP)).astype(bf16)
        high, low = split(merged[...])
        blocks = mm(chosen, high) + mm(chosen, low)
        owner = lax.broadcasted_iota(jnp.int32, (owners, 1), 0)
        bottom = owner * rows_dev
        lane = lax.broadcasted_iota(jnp.int32, (owners, LANES), 1)
        meta = jnp.zeros((owners, LANES), f32)
        for ids, count, base in ((listed, CAP, 0), (wanted, RCAP, CAP)):
            size = ids.shape[1]
            below = ids < bottom
            inside = jnp.logical_not(below) & (ids < bottom + rows_dev)
            start = jnp.sum(below.astype(f32), axis=1, keepdims=True).astype(jnp.int32)
            at = lax.broadcasted_iota(jnp.int32, (owners, size), 1) - start
            local = (ids - bottom - rows_dev).astype(f32)
            for k in range(count):
                value = jnp.sum(
                    jnp.where(inside & (at == k), local, 0.0), axis=1, keepdims=True
                )
                meta = jnp.where(lane == base + k, value + float(rows_dev), meta)
        payload[...] = blocks
        payload[pl.ds(CAP, owners, stride=SLOT), :] = meta


def update_kernel(recv, table, accum, new_table, new_accum, answers, metas, ids, old, olda, new, sem):
    owners = recv.shape[0] // SLOT
    rows = table.shape[0]
    count = owners * CAP
    meta = recv[pl.ds(CAP, owners, stride=SLOT), :]
    metas[...] = meta.astype(jnp.int32)
    copy = pltpu.make_async_copy(metas, ids, sem)
    copy.start()
    new_table[...] = table[...]
    grads = jnp.concatenate(
        [recv[pl.ds(k, owners, stride=SLOT), :] for k in range(CAP)], axis=0
    )
    col = jnp.concatenate([meta[:, k : k + 1] for k in range(CAP)], axis=0)
    eye = lax.broadcasted_iota(jnp.int32, (count, count), 0)
    eye_t = lax.broadcasted_iota(jnp.int32, (count, count), 1)
    line = jnp.sum(jnp.where(eye == eye_t, col, 0.0), axis=0, keepdims=True)
    same = (col == line).astype(f32)
    total = jnp.dot(
        same, grads, precision=lax.Precision.HIGHEST, preferred_element_type=f32
    )
    earlier = jnp.sum(jnp.where(eye_t < eye, same, 0.0), axis=1, keepdims=True)
    square = jnp.mean(total * total, axis=1, keepdims=True)
    copy.wait()

    def take(o, carry):
        for k in range(CAP):
            r = jnp.minimum(ids[o, k], rows - 1)
            old[pl.ds(k * owners + o, 1), :] = table[pl.ds(r, 1), :]
            olda[pl.ds(k * owners + o, 1), :] = accum[pl.ds(r // LANES, 1), :]
        return carry

    lax.fori_loop(0, owners, take, 0)
    number = col.astype(jnp.int32)
    lane = lax.broadcasted_iota(jnp.int32, (count, LANES), 1)
    mine = lane == number % LANES
    before = jnp.sum(jnp.where(mine, olda[...], 0.0), axis=1, keepdims=True)
    new[...] = old[...] - RATE * total / (jnp.sqrt(before + square) + EPS)

    counted = mine & (earlier == 0.0) & (col < float(rows))
    place = jnp.where(counted, square, 0.0)
    lines = accum.shape[0]
    row_hot = (
        lax.broadcasted_iota(jnp.int32, (lines, count), 0) == line.astype(jnp.int32) // LANES
    ).astype(f32)
    new_accum[...] = accum[...] + jnp.dot(
        row_hot, place, precision=lax.Precision.HIGHEST, preferred_element_type=f32
    )

    def put(o, carry):
        for k in range(CAP):
            r = ids[o, k]

            @pl.when(r < rows)
            def _():
                new_table[pl.ds(r, 1), :] = new[pl.ds(k * owners + o, 1), :]

        return carry

    lax.fori_loop(0, owners, put, 0)

    def answer(o, carry):
        for k in range(RCAP):
            r = jnp.minimum(ids[o, CAP + k], rows - 1)
            answers[pl.ds(o * RCAP + k, 1), :] = new_table[pl.ds(r, 1), :]
        return carry

    lax.fori_loop(0, owners, answer, 0)


def local(
    embeddings,
    cot_first,
    cot_second,
    cot_third,
    w_first,
    w_second,
    w_third,
    unique_ids,
    inverse,
    table,
    accum,
    next_ids,
):
    samples, fields, embed = embeddings.shape
    maps = w_first.shape[0]
    fp = up(fields + 1, SUB)
    hp = up(maps, SUB)
    pairs = fp // 2
    fb = fp // SUB
    width = BLOCK * embed
    owners = lax.axis_size("group") * lax.axis_size("member")
    rows_dev = table.shape[0]
    unique = unique_ids.shape[1]
    steps = samples // BLOCK

    emb_t = jnp.transpose(embeddings, (1, 0, 2))
    w1 = jnp.transpose(w_first, (1, 2, 0)).astype(f32)
    w1 = (w1 + jnp.swapaxes(w1, 0, 1)).astype(bf16)
    w1 = jnp.pad(w1, ((0, fp - fields), (0, fp - fields), (0, LANES - maps)))
    pad = ((0, fp - fields), (0, LANES - maps), (0, LANES - maps))
    w2 = jnp.pad(jnp.transpose(w_second, (2, 0, 1)), pad)
    w3 = jnp.pad(jnp.transpose(w_third, (2, 0, 1)), pad)

    p1_rows = sum(4 * PACK * (fb - b) for b in range(fb))
    p2_rows = pairs * 2 * hp
    vmem = pl.BlockSpec(memory_space=pltpu.VMEM)
    payload = pl.pallas_call(
        functools.partial(grad_kernel, fields, rows_dev),
        grid=(steps,),
        out_shape=jax.ShapeDtypeStruct((owners * SLOT, embed), f32),
        in_specs=[vmem] * 10,
        out_specs=vmem,
        scratch_shapes=[
            pltpu.VMEM((fp * samples, LANES), f32),
            pltpu.VMEM((fp * samples, LANES), f32),
            pltpu.VMEM((samples, LANES), bf16),
            pltpu.VMEM((samples, LANES), bf16),
            pltpu.VMEM((up(p1_rows, LANES), LANES), bf16),
            pltpu.VMEM((hp, up(p1_rows, LANES)), bf16),
            pltpu.VMEM((up(p2_rows, LANES), LANES), bf16),
            pltpu.VMEM((hp, up(p2_rows, LANES)), bf16),
            pltpu.VMEM((fp, width), f32),
            pltpu.VMEM((pairs, PACK, width), bf16),
            pltpu.VMEM((p1_rows, width), bf16),
            pltpu.VMEM((p2_rows, width), bf16),
            pltpu.VMEM((hp, width), f32),
            pltpu.VMEM((LANES, width), bf16),
            pltpu.VMEM((LANES, width), bf16),
            pltpu.VMEM((LANES, width), bf16),
            pltpu.VMEM((hp, width), f32),
            pltpu.VMEM((BLOCK * fp * SUB, LANES), f32),
            pltpu.VMEM((fp, width), f32),
            pltpu.VMEM((unique, LANES), f32),
        ],
        compiler_params=pltpu.CompilerParams(vmem_limit_bytes=48 * 2**20),
        name="gradients",
    )(emb_t, cot_first, cot_second, cot_third, w1, w2, w3, unique_ids, next_ids, inverse)

    axes = ("group", "member")
    recv = lax.all_to_all(payload, axes, split_axis=0, concat_axis=0, tiled=True)
    lines = rows_dev // LANES
    new_table, new_accum, answers = pl.pallas_call(
        update_kernel,
        out_shape=(
            jax.ShapeDtypeStruct((rows_dev, embed), f32),
            jax.ShapeDtypeStruct((lines, LANES), f32),
            jax.ShapeDtypeStruct((owners * RCAP, embed), f32),
        ),
        in_specs=[vmem] * 3,
        out_specs=(vmem,) * 3,
        scratch_shapes=[
            pltpu.VMEM((owners, LANES), jnp.int32),
            pltpu.SMEM((owners, LANES), jnp.int32),
            pltpu.VMEM((owners * CAP, LANES), f32),
            pltpu.VMEM((owners * CAP, LANES), f32),
            pltpu.VMEM((owners * CAP, LANES), f32),
            pltpu.SemaphoreType.DMA,
        ],
        compiler_params=pltpu.CompilerParams(vmem_limit_bytes=48 * 2**20),
        name="update",
    )(recv, table, accum.reshape(lines, LANES))
    back = lax.all_to_all(answers, axes, split_axis=0, concat_axis=0, tiled=True)

    wanted = next_ids[0]
    owner_of = wanted // rows_dev
    leading = jnp.sum((owner_of[None, :] < owner_of[:, None]).astype(jnp.int32), axis=1)
    within = jnp.arange(wanted.shape[0], dtype=jnp.int32) - leading
    returned = back[owner_of * RCAP + within]
    return (new_table, new_accum.reshape(rows_dev), returned[None])


def solution(mesh):
    both = ("group", "member")
    in_specs = (
        P(both, None, None),
        P(both, None),
        P(both, None),
        P(both, None),
        P(),
        P(),
        P(),
        P(both, None),
        P(both, None),
        P(both, None),
        P(both),
        P(both, None),
    )
    out_specs = (P(both, None), P(both), P(both, None, None))
    return jax.shard_map(local, mesh=mesh, in_specs=in_specs, out_specs=out_specs, check_vma=False)
```

```python
import functools

import jax
import jax.numpy as jnp
from jax import lax
from jax.experimental import pallas as pl
from jax.experimental.pallas import tpu as pltpu
from jax.sharding import PartitionSpec as P

CAP = 4
RCAP = 8

RATE = 0.5
EPS = 1e-08

LANES = 128
SUB = 8
PACK = 16
SLOT = 8
TILE = 256
BLOCK = 8

f32 = jnp.float32
bf16 = jnp.bfloat16


def up(value, unit):
    return -(-value // unit) * unit


def split(value):
    high = value.astype(bf16)
    return high, (value - high.astype(f32)).astype(bf16)


def mm(a, b):
    return jnp.dot(a, b, preferred_element_type=f32)


def mm_t(a, b):
    return lax.dot_general(a, b, (((0,), (0,)), ((), ())), preferred_element_type=f32)


def grad_kernel(
    fields,
    rows_dev,
    emb_in,
    c1_in,
    c2_in,
    c3_in,
    w1_in,
    w2_in,
    w3_in,
    uid_in,
    nid_in,
    inv_in,
    payload,
    emb,
    c1,
    c2,
    c3,
    w1,
    w2,
    w3,
    uid,
    nid,
    inv,
    sems,
    xs,
    top,
    c1s,
    c3s,
    w1f,
    w2f,
    w3f,
    w1s,
    w1t,
    w2s,
    w2t,
    xf,
    xp,
    dy,
    p1,
    p2,
    y1s,
    y2s,
    us,
    ls,
    acc,
    part,
    grad,
    gs,
):
    step = pl.program_id(0)
    samples = inv.shape[0]
    maps = c1.shape[1]
    fp = xf.shape[0]
    hp = acc.shape[0]
    hb = hp // SUB
    fb = fp // SUB
    pairs = fp // 2
    width = xf.shape[1]

    def offsets():
        place = 0
        for m in range(pairs):
            ib = (2 * m) // SUB
            for jb in range(ib, fb):
                yield m, ib, jb, place
                place += PACK

    sources = (emb_in, c1_in, c2_in, c3_in, w1_in, w2_in, w3_in, uid_in, nid_in, inv_in)
    targets = (emb, c1, c2, c3, w1, w2, w3, uid, nid, inv)

    def fetch(q):
        return pltpu.make_async_copy(sources[q], targets[q], sems.at[q])

    @pl.when(step == 0)
    def _():
        for q in (6, 3, 2, 1, 5, 4, 0, 9, 7, 8):
            fetch(q).start()
        us[...] = jnp.zeros_like(us)
        ls[...] = jnp.zeros_like(ls)
        y2s[...] = jnp.zeros_like(y2s)
        part[...] = jnp.zeros_like(part)
        w1s[...] = jnp.zeros_like(w1s)
        w1f[...] = jnp.zeros_like(w1f)
        w2f[...] = jnp.zeros_like(w2f)
        w3f[...] = jnp.zeros_like(w3f)
        c1s[...] = jnp.zeros_like(c1s)
        c3s[...] = jnp.zeros_like(c3s)
        fetch(6).wait()
        for h in range(maps):
            w3f[pl.ds(h * fp, fields), 0:maps] = w3[h].astype(f32)
        fetch(3).wait()
        c3s[:, 0:maps] = c3[...]
        for j in range(fields):
            top[pl.ds(j * samples, samples), :] = mm(
                c3s[:, 0:hp], w3f[pl.ds(j, hp, stride=fp), :].astype(bf16)
            )
        top[pl.ds(fields * samples, samples), :] = jnp.zeros((samples, LANES), f32)
        fetch(2).wait()
        top[pl.ds(fields * samples, samples), 0:maps] = c2[...].astype(f32)
        fetch(1).wait()
        c1s[:, 0:maps] = c1[...]
        fetch(5).wait()
        for h in range(maps):
            w2f[pl.ds(h * fp, fields), 0:maps] = w2[h].astype(f32)
        for m in range(pairs):
            two = []
            for s in range(2):
                flat = w2f[pl.ds(2 * m + s, hp, stride=fp), :]
                flat = jnp.concatenate([flat, jnp.zeros((LANES - hp, LANES), f32)], axis=0)
                two.append(flat.T[0:hp].reshape(hb, SUB, LANES))
            w2s[pl.ds(m * 2 * hp, 2 * hp), :] = (
                jnp.stack(two, axis=1).reshape(2 * hp, LANES).astype(bf16)
            )
        w2s[pl.ds(pairs * 2 * hp, w2s.shape[0] - pairs * 2 * hp), :] = jnp.zeros(
            (w2s.shape[0] - pairs * 2 * hp, LANES), bf16
        )
        for c in range(w2s.shape[0] // LANES):
            w2t[:, c * LANES : (c + 1) * LANES] = (
                w2s[c * LANES : (c + 1) * LANES, :].astype(f32).T[0:hp].astype(bf16)
            )
        fetch(4).wait()
        for i in range(fields):
            w1f[pl.ds(i * fp, fields), 0:maps] = w1[i].astype(f32)
        for m, ib, jb, place in offsets():
            two = []
            for s in range(2):
                i = 2 * m + s
                direct = w1f[pl.ds(i * fp + SUB * jb, SUB), :]
                two.append(direct + w1f[pl.ds(SUB * jb * fp + i, SUB, stride=fp), :])
            w1s[pl.ds(place, PACK), :] = jnp.concatenate(two, axis=0).astype(bf16)
        for c in range(w1s.shape[0] // LANES):
            w1t[:, c * LANES : (c + 1) * LANES] = (
                w1s[c * LANES : (c + 1) * LANES, :].astype(f32).T[0:hp].astype(bf16)
            )
        fetch(0).wait()
        xs[pl.ds(0, fields * samples), :] = (
            emb[...].astype(f32).reshape(fields * samples, LANES)
        )
        xs[pl.ds(fields * samples, samples), :] = jnp.zeros((samples, LANES), f32)
        fetch(9).wait()
        fetch(7).wait()
        fetch(8).wait()

    first = step * BLOCK
    for k in range(BLOCK):
        xf[:, k * LANES : (k + 1) * LANES] = xs[pl.ds(first + k, fp, stride=samples), :]
    for m in range(pairs):
        xp[m] = jnp.concatenate(
            [jnp.broadcast_to(xf[2 * m + s : 2 * m + s + 1, :], (SUB, width)) for s in range(2)],
            axis=0,
        ).astype(bf16)
    twice = []
    for b in range(fb):
        block = xf[SUB * b : SUB * (b + 1), :]
        twice.append(jnp.concatenate([block, block], axis=0).astype(bf16))
    half = [t * jnp.asarray(0.5, bf16) for t in twice]
    for m, ib, jb, place in offsets():
        p1[pl.ds(place, PACK), :] = xp[m] * (half[jb] if jb == ib else twice[jb])
    layer_one = mm(w1t[:, 0 : p1.shape[0]], p1[...]).astype(bf16).astype(f32)
    y1s[...] = layer_one
    for b in range(hb):
        block = y1s[SUB * b : SUB * (b + 1), :]
        dy[b] = jnp.concatenate([block, block], axis=0).astype(bf16)
    for m in range(pairs):
        for b in range(hb):
            p2[pl.ds(m * 2 * hp + b * PACK, PACK), :] = xp[m] * dy[b]
    y2s[0:hp, :] = mm(w2t[:, 0 : p2.shape[0]], p2[...]).astype(bf16)

    last_row = lax.broadcasted_iota(jnp.int32, (fp, LANES), 0) == fields
    tops = []
    for k in range(BLOCK):
        here = slice(k * LANES, (k + 1) * LANES)
        high, low = split(top[pl.ds(first + k, fp, stride=samples), :])
        tops.append((high, low))
        own = jnp.where(last_row, 1.0, xf[:, here]).astype(bf16)
        us[:, here] = mm_t(
            jnp.concatenate([high, low], axis=0), jnp.concatenate([own, own], axis=0)
        ).astype(bf16)

    pick = (
        lax.broadcasted_iota(jnp.int32, (samples, width), 0)
        == first + lax.broadcasted_iota(jnp.int32, (samples, width), 1) // LANES
    )
    acc[...] = mm_t(c1s[...], pick.astype(bf16))[0:hp]
    group = 2
    for cut in range(0, width, TILE):
        cols = slice(cut, cut + TILE)
        samples_here = range(cut // LANES, (cut + TILE) // LANES)
        for m0 in range(0, pairs, group):
            z = mm(w2s[m0 * 2 * hp : (m0 + group) * 2 * hp, :], us[:, cols])
            js = range(2 * m0, 2 * (m0 + group))
            factors = [xf[j : j + 1, cols] for j in js]
            sums = [None] * len(js)
            for b in range(hb):
                rows = slice(SUB * b, SUB * (b + 1))
                one = y1s[rows, cols]
                total = acc[rows, cols]
                for q, j in enumerate(js):
                    at = (q // 2) * 2 * hp + b * PACK + (q % 2) * SUB
                    zj = z[at : at + SUB]
                    if j < fields:
                        total = total + zj * factors[q]
                        term = zj * one
                        sums[q] = term if sums[q] is None else sums[q] + term
                acc[rows, cols] = total
            for q, j in enumerate(js):
                if j < fields:
                    for k in samples_here:
                        part[pl.ds((k * fp + j) * SUB, SUB), :] = sums[q][
                            :, k * LANES - cut : (k + 1) * LANES - cut
                        ]
    ls[0:hp, :] = acc[...].astype(bf16)

    for cut in range(0, width, TILE):
        cols = slice(cut, cut + TILE)
        samples_here = range(cut // LANES, (cut + TILE) // LANES)
        z = mm(w1s[0 : p1.shape[0], :], ls[:, cols])
        totals = [None] * fb
        for m in range(pairs):
            ib = (2 * m) // SUB
            place = [q for q in offsets() if q[0] == m]
            for s in range(2):
                i = 2 * m + s
                if i >= fields:
                    continue
                factor = xf[i : i + 1, cols]
                across = None
                for _, _, jb, at in place:
                    zj = z[at + SUB * s : at + SUB * (s + 1)]
                    term = zj * factor
                    totals[jb] = term if totals[jb] is None else totals[jb] + term
                    if jb > ib:
                        term = zj * xf[SUB * jb : SUB * (jb + 1), cols]
                        across = term if across is None else across + term
                if across is not None:
                    for k in samples_here:
                        part[pl.ds((k * fp + i) * SUB, SUB), :] += across[
                            :, k * LANES - cut : (k + 1) * LANES - cut
                        ]
        for jb in range(fb):
            grad[SUB * jb : SUB * (jb + 1), cols] = totals[jb]

    for k in range(BLOCK):
        here = slice(k * LANES, (k + 1) * LANES)
        mine = grad[:, here]
        for s in range(SUB):
            mine = mine + part[pl.ds(k * fp * SUB + s, fp, stride=SUB), :]
        high, low = tops[k]
        y2 = y2s[:, here]
        gs[pl.ds((first + k) * fp, fp), :] = mine + mm(
            jnp.concatenate([high, low], axis=1), jnp.concatenate([y2, y2], axis=0)
        )

    @pl.when(step == pl.num_programs(0) - 1)
    def _():
        owners = payload.shape[0] // SLOT
        rows = owners * SLOT
        positions = uid.shape[1]
        named = []
        for n in range(samples):
            named.append(inv[n : n + 1, :])
            named.append(jnp.full((1, fp - fields), -1, jnp.int32))
        named = jnp.concatenate(named, axis=1)
        chosen = (
            lax.broadcasted_iota(jnp.int32, (positions, samples * fp), 0)
            == jnp.broadcast_to(named, (positions, samples * fp))
        ).astype(bf16)
        high, low = split(gs[...])
        merged = mm(chosen, high) + mm(chosen, low)

        listed = uid[...]
        wanted = nid[...]
        row = lax.broadcasted_iota(jnp.int32, (rows, 1), 0)
        owner = row // SLOT
        slot = row % SLOT
        bottom = owner * rows_dev
        start = jnp.sum((listed < bottom).astype(f32), axis=1, keepdims=True).astype(jnp.int32)
        at = lax.broadcasted_iota(jnp.int32, (rows, positions), 1)
        inside = (listed >= bottom) & (listed < bottom + rows_dev)
        chosen = ((at == start + slot) & inside & (slot < CAP)).astype(bf16)
        high, low = split(merged)
        blocks = mm(chosen, high) + mm(chosen, low)
        owner = lax.broadcasted_iota(jnp.int32, (owners, 1), 0)
        bottom = owner * rows_dev
        lane = lax.broadcasted_iota(jnp.int32, (owners, LANES), 1)
        meta = jnp.zeros((owners, LANES), f32)
        for ids, count, base in ((listed, CAP, 0), (wanted, RCAP, CAP)):
            size = ids.shape[1]
            below = ids < bottom
            inside = jnp.logical_not(below) & (ids < bottom + rows_dev)
            start = jnp.sum(below.astype(f32), axis=1, keepdims=True).astype(jnp.int32)
            at = lax.broadcasted_iota(jnp.int32, (owners, size), 1) - start
            local = (ids - bottom - rows_dev).astype(f32)
            for k in range(count):
                value = jnp.sum(
                    jnp.where(inside & (at == k), local, 0.0), axis=1, keepdims=True
                )
                meta = jnp.where(lane == base + k, value + float(rows_dev), meta)
        payload[...] = blocks
        payload[pl.ds(CAP, owners, stride=SLOT), :] = meta


def picked(mask, value):
    high, low = split(value)
    rest = (value - high.astype(f32) - low.astype(f32)).astype(bf16)
    mask = mask.astype(bf16)
    return mm(
        jnp.concatenate([mask, mask, mask], axis=1),
        jnp.concatenate([high, low, rest], axis=0),
    )


def numbers(meta, owners, count, base):
    size = owners * count
    col = jnp.concatenate([meta[:, base + k : base + k + 1] for k in range(count)], axis=0)
    down = lax.broadcasted_iota(jnp.int32, (size, size), 0)
    along = lax.broadcasted_iota(jnp.int32, (size, size), 1)
    line = jnp.sum(jnp.where(down == along, col, 0.0), axis=0, keepdims=True)
    same = col == line
    earlier = jnp.sum(jnp.where(same & (down < along), 1.0, 0.0), axis=0, keepdims=True)
    return col, line, same, earlier == 0.0


def update_kernel(recv, table, accum, answers, new, place, metas, ids, old, olda, found, sem):
    owners = recv.shape[0] // SLOT
    rows = table.shape[0]
    count = owners * CAP
    meta = recv[pl.ds(CAP, owners, stride=SLOT), :]
    metas[...] = meta.astype(jnp.int32)
    copy = pltpu.make_async_copy(metas, ids, sem)
    copy.start()
    grads = jnp.concatenate(
        [recv[pl.ds(k, owners, stride=SLOT), :] for k in range(CAP)], axis=0
    )
    col, line, same, once = numbers(meta, owners, CAP, 0)
    total = picked(same, grads)
    square = jnp.mean(total * total, axis=1, keepdims=True)
    valid = once & (line < float(rows))
    asks = jnp.concatenate([meta[:, CAP + k : CAP + k + 1] for k in range(RCAP)], axis=0)
    match = (asks == line) & valid
    hit = jnp.max(match.astype(f32), axis=1, keepdims=True) > 0.0
    copy.wait()

    def take(o, carry):
        for k in range(CAP):
            r = jnp.minimum(ids[o, k], rows - 1)
            old[pl.ds(k * owners + o, 1), :] = table[pl.ds(r, 1), :]
            olda[pl.ds(k * owners + o, 1), :] = accum[pl.ds(r // LANES, 1), :]
        for k in range(RCAP):
            r = jnp.minimum(ids[o, CAP + k], rows - 1)
            found[pl.ds(k * owners + o, 1), :] = table[pl.ds(r, 1), :]
        return carry

    lax.fori_loop(0, owners, take, 0, unroll=4)
    lane = lax.broadcasted_iota(jnp.int32, (count, LANES), 1)
    mine = lane == col.astype(jnp.int32) % LANES
    before = jnp.sum(jnp.where(mine, olda[...], 0.0), axis=1, keepdims=True)
    after = old[...] - RATE * total / (jnp.sqrt(before + square) + EPS)
    new[...] = after
    place[...] = jnp.where(mine, square, 0.0)
    out = jnp.where(hit, picked(match, after), found[...])
    for k in range(RCAP):
        answers[pl.ds(k, owners, stride=RCAP), :] = out[k * owners : (k + 1) * owners]


def store_kernel(recv, table, accum, new, place, new_table, new_accum, metas, ids, sem):
    owners = recv.shape[0] // SLOT
    rows = table.shape[0]
    count = owners * CAP
    meta = recv[pl.ds(CAP, owners, stride=SLOT), :]
    metas[...] = meta.astype(jnp.int32)
    copy = pltpu.make_async_copy(metas, ids, sem)
    copy.start()
    new_table[...] = table[...]
    _, line, _, once = numbers(meta, owners, CAP, 0)
    lines = accum.shape[0]
    row_hot = (
        lax.broadcasted_iota(jnp.int32, (lines, count), 0) == line.astype(jnp.int32) // LANES
    ) & (once & (line < float(rows)))
    new_accum[...] = accum[...] + picked(row_hot, place[...])
    copy.wait()

    def put(o, carry):
        for k in range(CAP):
            r = ids[o, k]

            @pl.when(r < rows)
            def _():
                new_table[pl.ds(r, 1), :] = new[pl.ds(k * owners + o, 1), :]

        return carry

    lax.fori_loop(0, owners, put, 0)


def gradients(
    owners,
    rows_dev,
    embeddings,
    cot_first,
    cot_second,
    cot_third,
    w_first,
    w_second,
    w_third,
    unique_ids,
    inverse,
    next_ids,
):
    samples, fields, embed = embeddings.shape
    maps = w_first.shape[0]
    fp = up(fields + 1, SUB)
    hp = up(maps, SUB)
    pairs = fp // 2
    fb = fp // SUB
    width = BLOCK * embed
    steps = samples // BLOCK

    emb_t = jnp.transpose(embeddings, (1, 0, 2))
    w1 = jnp.transpose(w_first, (1, 2, 0))
    w2 = jnp.transpose(w_second, (0, 2, 1))
    w3 = jnp.transpose(w_third, (0, 2, 1))

    arrays = (
        emb_t, cot_first, cot_second, cot_third, w1, w2, w3, unique_ids, next_ids, inverse
    )
    p1_rows = sum(4 * PACK * (fb - b) for b in range(fb))
    p2_rows = pairs * 2 * hp
    vmem = pl.BlockSpec(memory_space=pltpu.VMEM)
    return pl.pallas_call(
        functools.partial(grad_kernel, fields, rows_dev),
        grid=(steps,),
        out_shape=jax.ShapeDtypeStruct((owners * SLOT, embed), f32),
        in_specs=[pl.BlockSpec(memory_space=pl.ANY)] * 10,
        out_specs=vmem,
        scratch_shapes=[pltpu.VMEM(a.shape, a.dtype) for a in arrays]
        + [
            pltpu.SemaphoreType.DMA((len(arrays),)),
            pltpu.VMEM((fp * samples, LANES), f32),
            pltpu.VMEM((fp * samples, LANES), f32),
            pltpu.VMEM((samples, LANES), bf16),
            pltpu.VMEM((samples, LANES), bf16),
            pltpu.VMEM((fp * fp, LANES), f32),
            pltpu.VMEM((hp * fp, LANES), f32),
            pltpu.VMEM((hp * fp, LANES), f32),
            pltpu.VMEM((up(p1_rows, LANES), LANES), bf16),
            pltpu.VMEM((hp, up(p1_rows, LANES)), bf16),
            pltpu.VMEM((up(p2_rows, LANES), LANES), bf16),
            pltpu.VMEM((hp, up(p2_rows, LANES)), bf16),
            pltpu.VMEM((fp, width), f32),
            pltpu.VMEM((pairs, PACK, width), bf16),
            pltpu.VMEM((hp // SUB, PACK, width), bf16),
            pltpu.VMEM((p1_rows, width), bf16),
            pltpu.VMEM((p2_rows, width), bf16),
            pltpu.VMEM((hp, width), f32),
            pltpu.VMEM((LANES, width), bf16),
            pltpu.VMEM((LANES, width), bf16),
            pltpu.VMEM((LANES, width), bf16),
            pltpu.VMEM((hp, width), f32),
            pltpu.VMEM((BLOCK * fp * SUB, LANES), f32),
            pltpu.VMEM((fp, width), f32),
            pltpu.VMEM((samples * fp, LANES), f32),
        ],
        compiler_params=pltpu.CompilerParams(vmem_limit_bytes=56 * 2**20),
        name="gradients",
    )(*arrays)


def local(
    embeddings,
    cot_first,
    cot_second,
    cot_third,
    w_first,
    w_second,
    w_third,
    unique_ids,
    inverse,
    table,
    accum,
    next_ids,
):
    owners = lax.axis_size("group") * lax.axis_size("member")
    rows_dev, embed = table.shape
    vmem = pl.BlockSpec(memory_space=pltpu.VMEM)
    payload = gradients(
        owners,
        rows_dev,
        embeddings,
        cot_first,
        cot_second,
        cot_third,
        w_first,
        w_second,
        w_third,
        unique_ids,
        inverse,
        next_ids,
    )
    axes = ("group", "member")
    recv = lax.all_to_all(payload, axes, split_axis=0, concat_axis=0, tiled=True)
    lines = rows_dev // LANES
    accum = accum.reshape(lines, LANES)
    answers, new, place = pl.pallas_call(
        update_kernel,
        out_shape=(
            jax.ShapeDtypeStruct((owners * RCAP, embed), f32),
            jax.ShapeDtypeStruct((owners * CAP, embed), f32),
            jax.ShapeDtypeStruct((owners * CAP, embed), f32),
        ),
        in_specs=[vmem] * 3,
        out_specs=(vmem,) * 3,
        scratch_shapes=[
            pltpu.VMEM((owners, LANES), jnp.int32),
            pltpu.SMEM((owners, LANES), jnp.int32),
            pltpu.VMEM((owners * CAP, LANES), f32),
            pltpu.VMEM((owners * CAP, LANES), f32),
            pltpu.VMEM((owners * RCAP, LANES), f32),
            pltpu.SemaphoreType.DMA,
        ],
        compiler_params=pltpu.CompilerParams(vmem_limit_bytes=48 * 2**20),
        name="update",
    )(recv, table, accum)
    back = lax.all_to_all(answers, axes, split_axis=0, concat_axis=0, tiled=True)
    new_table, new_accum = pl.pallas_call(
        store_kernel,
        out_shape=(
            jax.ShapeDtypeStruct((rows_dev, embed), f32),
            jax.ShapeDtypeStruct((lines, LANES), f32),
        ),
        in_specs=[vmem] * 5,
        out_specs=(vmem,) * 2,
        scratch_shapes=[
            pltpu.VMEM((owners, LANES), jnp.int32),
            pltpu.SMEM((owners, LANES), jnp.int32),
            pltpu.SemaphoreType.DMA,
        ],
        compiler_params=pltpu.CompilerParams(vmem_limit_bytes=48 * 2**20),
        cost_estimate=pl.CostEstimate(
            flops=2 * lines * 3 * owners * CAP * LANES,
            bytes_accessed=2 * rows_dev * embed * 4,
            transcendentals=0,
        ),
        name="store",
    )(recv, table, accum, new, place)

    wanted = next_ids[0]
    owner_of = wanted // rows_dev
    leading = jnp.sum((owner_of[None, :] < owner_of[:, None]).astype(jnp.int32), axis=1)
    within = jnp.arange(wanted.shape[0], dtype=jnp.int32) - leading
    returned = back[owner_of * RCAP + within]
    return (new_table, new_accum.reshape(rows_dev), returned[None])


def solution(mesh):
    both = ("group", "member")
    in_specs = (
        P(both, None, None),
        P(both, None),
        P(both, None),
        P(both, None),
        P(),
        P(),
        P(),
        P(both, None),
        P(both, None),
        P(both, None),
        P(both),
        P(both, None),
    )
    out_specs = (P(both, None), P(both), P(both, None, None))
    return jax.shard_map(local, mesh=mesh, in_specs=in_specs, out_specs=out_specs, check_vma=False)
```

```python
import functools

import jax
import jax.numpy as jnp
from jax import lax
from jax.experimental import pallas as pl
from jax.experimental.pallas import tpu as pltpu
from jax.sharding import PartitionSpec as P

CAP = 4
RCAP = 8

RATE = 0.5
EPS = 1e-08

LANES = 128
SUB = 8
PACK = 16
SLOT = 8
TILE = 256
BLOCK = 16

f32 = jnp.float32
bf16 = jnp.bfloat16


def up(value, unit):
    return -(-value // unit) * unit


def split(value):
    high = value.astype(bf16)
    return high, (value - high.astype(f32)).astype(bf16)


def mm(a, b):
    return jnp.dot(a, b, preferred_element_type=f32)


def mm_t(a, b):
    return lax.dot_general(a, b, (((0,), (0,)), ((), ())), preferred_element_type=f32)


def grad_kernel(
    fields,
    rows_dev,
    emb_in,
    c1_in,
    c2_in,
    c3_in,
    w1_in,
    w2_in,
    w3_in,
    uid_in,
    nid_in,
    inv_in,
    payload,
    emb,
    c1,
    c2,
    c3,
    w1,
    w2,
    w3,
    uid,
    nid,
    inv,
    sems,
    xs,
    top,
    c1s,
    c3s,
    w1f,
    w2f,
    w3f,
    w1s,
    w1t,
    w2s,
    w2t,
    xf,
    xp,
    dy,
    p1,
    p2,
    y1s,
    y2s,
    us,
    ls,
    acc,
    part,
    grad,
    gs,
):
    step = pl.program_id(0)
    samples = inv.shape[0]
    maps = c1.shape[1]
    fp = xf.shape[0]
    hp = acc.shape[0]
    hb = hp // SUB
    fb = fp // SUB
    pairs = fp // 2
    full = fields // 2
    width = xf.shape[1]

    def stacked(j, b):
        if j < 2 * full:
            return (j // 2) * 2 * hp + b * PACK + (j % 2) * SUB
        return full * 2 * hp + b * SUB

    def offsets():
        place = 0
        for m in range(pairs):
            ib = (2 * m) // SUB
            for jb in range(ib, fb):
                yield m, ib, jb, place
                place += PACK

    sources = (emb_in, c1_in, c2_in, c3_in, w1_in, w2_in, w3_in, uid_in, nid_in, inv_in)
    targets = (emb, c1, c2, c3, w1, w2, w3, uid, nid, inv)

    def fetch(q):
        return pltpu.make_async_copy(sources[q], targets[q], sems.at[q])

    @pl.when(step == 0)
    def _():
        for q in (0, 4, 3, 2, 1, 6, 5, 9, 7, 8):
            fetch(q).start()
        us[...] = jnp.zeros_like(us)
        ls[...] = jnp.zeros_like(ls)
        y2s[...] = jnp.zeros_like(y2s)
        part[...] = jnp.zeros_like(part)
        w1s[...] = jnp.zeros_like(w1s)
        w1f[...] = jnp.zeros_like(w1f)
        w2f[...] = jnp.zeros_like(w2f)
        w3f[...] = jnp.zeros_like(w3f)
        c1s[...] = jnp.zeros_like(c1s)
        c3s[...] = jnp.zeros_like(c3s)
        fetch(0).wait()
        xs[pl.ds(0, fields * samples), :] = (
            emb[...].astype(f32).reshape(fields * samples, LANES)
        )
        xs[pl.ds(fields * samples, samples), :] = jnp.zeros((samples, LANES), f32)
        fetch(4).wait()
        for i in range(fields):
            w1f[pl.ds(i * fp, fields), 0:maps] = w1[i].astype(f32)
        for m, ib, jb, place in offsets():
            two = []
            for s in range(2):
                i = 2 * m + s
                direct = w1f[pl.ds(i * fp + SUB * jb, SUB), :]
                two.append(direct + w1f[pl.ds(SUB * jb * fp + i, SUB, stride=fp), :])
            w1s[pl.ds(place, PACK), :] = jnp.concatenate(two, axis=0).astype(bf16)
        for c in range(w1s.shape[0] // LANES):
            w1t[:, c * LANES : (c + 1) * LANES] = (
                w1s[c * LANES : (c + 1) * LANES, :].astype(f32).T[0:hp].astype(bf16)
            )
        fetch(6).wait()
        for h in range(maps):
            w3f[pl.ds(h * fp, fields), 0:maps] = w3[h].astype(f32)
        fetch(3).wait()
        c3s[:, 0:maps] = c3[...]
        for j in range(fields):
            top[pl.ds(j * samples, samples), :] = mm(
                c3s[:, 0:hp], w3f[pl.ds(j, hp, stride=fp), :].astype(bf16)
            )
        top[pl.ds(fields * samples, samples), :] = jnp.zeros((samples, LANES), f32)
        fetch(2).wait()
        top[pl.ds(fields * samples, samples), 0:maps] = c2[...].astype(f32)
        fetch(1).wait()
        c1s[:, 0:maps] = c1[...]
        fetch(5).wait()
        for h in range(maps):
            w2f[pl.ds(h * fp, fields), 0:maps] = w2[h].astype(f32)
        zeros = jnp.zeros((LANES - hp, LANES), f32)
        for m in range(full):
            two = []
            for s in range(2):
                flat = w2f[pl.ds(2 * m + s, hp, stride=fp), :]
                flat = jnp.concatenate([flat, zeros], axis=0)
                two.append(flat.T[0:hp].reshape(hb, SUB, LANES))
            w2s[pl.ds(m * 2 * hp, 2 * hp), :] = (
                jnp.stack(two, axis=1).reshape(2 * hp, LANES).astype(bf16)
            )
        rest = jnp.zeros((w2s.shape[0] - full * 2 * hp, LANES), f32)
        if fields % 2:
            flat = w2f[pl.ds(fields - 1, hp, stride=fp), :]
            flat = jnp.concatenate([flat, zeros], axis=0)
            rest = jnp.concatenate([flat.T[0:hp], rest[hp:]], axis=0)
        w2s[pl.ds(full * 2 * hp, rest.shape[0]), :] = rest.astype(bf16)
        for c in range(w2s.shape[0] // LANES):
            w2t[:, c * LANES : (c + 1) * LANES] = (
                w2s[c * LANES : (c + 1) * LANES, :].astype(f32).T[0:hp].astype(bf16)
            )
        fetch(9).wait()
        fetch(7).wait()
        fetch(8).wait()

    first = step * BLOCK
    for k in range(BLOCK):
        xf[:, k * LANES : (k + 1) * LANES] = xs[pl.ds(first + k, fp, stride=samples), :]
    for m in range(pairs):
        xp[m] = jnp.concatenate(
            [jnp.broadcast_to(xf[2 * m + s : 2 * m + s + 1, :], (SUB, width)) for s in range(2)],
            axis=0,
        ).astype(bf16)
    twice = []
    for b in range(fb):
        block = xf[SUB * b : SUB * (b + 1), :]
        twice.append(jnp.concatenate([block, block], axis=0).astype(bf16))
    half = [t * jnp.asarray(0.5, bf16) for t in twice]
    for m, ib, jb, place in offsets():
        p1[pl.ds(place, PACK), :] = xp[m] * (half[jb] if jb == ib else twice[jb])
    layer_one = mm(w1t[:, 0 : p1.shape[0]], p1[...]).astype(bf16).astype(f32)
    y1s[...] = layer_one
    for b in range(hb):
        block = y1s[SUB * b : SUB * (b + 1), :]
        dy[b] = jnp.concatenate([block, block], axis=0).astype(bf16)
    for m in range(full):
        for b in range(hb):
            p2[pl.ds(m * 2 * hp + b * PACK, PACK), :] = xp[m] * dy[b]
    if fields % 2:
        alone = jnp.broadcast_to(xf[fields - 1 : fields, :], (PACK, width)).astype(bf16)
        for b in range(0, hb, 2):
            block = y1s[SUB * b : SUB * min(b + 2, hb), :]
            if b + 1 == hb:
                block = jnp.concatenate([block, jnp.zeros_like(block)], axis=0)
            p2[pl.ds(full * 2 * hp + b * SUB, PACK), :] = alone * block.astype(bf16)
    y2s[0:hp, :] = mm(w2t[:, 0 : p2.shape[0]], p2[...]).astype(bf16)

    last_row = lax.broadcasted_iota(jnp.int32, (fp, LANES), 0) == fields
    for k in range(BLOCK):
        here = slice(k * LANES, (k + 1) * LANES)
        high, low = split(top[pl.ds(first + k, fp, stride=samples), :])
        own = jnp.where(last_row, 1.0, xf[:, here]).astype(bf16)
        us[:, here] = mm_t(
            jnp.concatenate([high, low], axis=0), jnp.concatenate([own, own], axis=0)
        ).astype(bf16)
        y2 = y2s[:, here]
        gs[pl.ds((first + k) * fp, fp), :] = mm(
            jnp.concatenate([high, low], axis=1), jnp.concatenate([y2, y2], axis=0)
        )

    pick = (
        lax.broadcasted_iota(jnp.int32, (samples, width), 0)
        == first + lax.broadcasted_iota(jnp.int32, (samples, width), 1) // LANES
    )
    acc[...] = mm_t(c1s[...], pick.astype(bf16))[0:hp]
    group = 20
    for cut in range(0, width, TILE):
        cols = slice(cut, cut + TILE)
        samples_here = range(cut // LANES, (cut + TILE) // LANES)
        for j0 in range(0, fields, 2 * group):
            js = range(j0, min(j0 + 2 * group, fields))
            base = stacked(j0, 0)
            z = mm(w2s[base : stacked(js[-1], hb - 1) + SUB, :], us[:, cols])
            factors = [xf[j : j + 1, cols] for j in js]
            sums = [None] * len(js)
            for b in range(hb):
                rows = slice(SUB * b, SUB * (b + 1))
                one = y1s[rows, cols]
                total = acc[rows, cols]
                for q, j in enumerate(js):
                    at = stacked(j, b) - base
                    zj = z[at : at + SUB]
                    total = total + zj * factors[q]
                    term = zj * one
                    sums[q] = term if sums[q] is None else sums[q] + term
                acc[rows, cols] = total
            for q, j in enumerate(js):
                for k in samples_here:
                    part[pl.ds((k * fp + j) * SUB, SUB), :] = sums[q][
                        :, k * LANES - cut : (k + 1) * LANES - cut
                    ]
    ls[0:hp, :] = acc[...].astype(bf16)

    for cut in range(0, width, TILE):
        cols = slice(cut, cut + TILE)
        samples_here = range(cut // LANES, (cut + TILE) // LANES)
        z = mm(w1s[0 : p1.shape[0], :], ls[:, cols])
        totals = [None] * fb
        for m in range(pairs):
            ib = (2 * m) // SUB
            place = [q for q in offsets() if q[0] == m]
            for s in range(2):
                i = 2 * m + s
                if i >= fields:
                    continue
                factor = xf[i : i + 1, cols]
                across = None
                for _, _, jb, at in place:
                    zj = z[at + SUB * s : at + SUB * (s + 1)]
                    term = zj * factor
                    totals[jb] = term if totals[jb] is None else totals[jb] + term
                    if jb > ib:
                        term = zj * xf[SUB * jb : SUB * (jb + 1), cols]
                        across = term if across is None else across + term
                if across is not None:
                    for k in samples_here:
                        part[pl.ds((k * fp + i) * SUB, SUB), :] += across[
                            :, k * LANES - cut : (k + 1) * LANES - cut
                        ]
        for jb in range(fb):
            grad[SUB * jb : SUB * (jb + 1), cols] = totals[jb]

    for k in range(BLOCK):
        here = slice(k * LANES, (k + 1) * LANES)
        mine = grad[:, here]
        for s in range(SUB):
            mine = mine + part[pl.ds(k * fp * SUB + s, fp, stride=SUB), :]
        gs[pl.ds((first + k) * fp, fp), :] += mine

    @pl.when(step == pl.num_programs(0) - 1)
    def _():
        owners = payload.shape[0] // SLOT
        rows = owners * SLOT
        positions = uid.shape[1]
        named = []
        for n in range(samples):
            named.append(inv[n : n + 1, :])
            named.append(jnp.full((1, fp - fields), -1, jnp.int32))
        named = jnp.concatenate(named, axis=1)
        chosen = (
            lax.broadcasted_iota(jnp.int32, (positions, samples * fp), 0)
            == jnp.broadcast_to(named, (positions, samples * fp))
        ).astype(bf16)
        high, low = split(gs[...])
        merged = mm(chosen, high) + mm(chosen, low)

        listed = uid[...]
        wanted = nid[...]
        row = lax.broadcasted_iota(jnp.int32, (rows, 1), 0)
        owner = row // SLOT
        slot = row % SLOT
        bottom = owner * rows_dev
        start = jnp.sum((listed < bottom).astype(f32), axis=1, keepdims=True).astype(jnp.int32)
        at = lax.broadcasted_iota(jnp.int32, (rows, positions), 1)
        inside = (listed >= bottom) & (listed < bottom + rows_dev)
        chosen = ((at == start + slot) & inside & (slot < CAP)).astype(bf16)
        high, low = split(merged)
        blocks = mm(chosen, high) + mm(chosen, low)
        owner = lax.broadcasted_iota(jnp.int32, (owners, 1), 0)
        bottom = owner * rows_dev
        lane = lax.broadcasted_iota(jnp.int32, (owners, LANES), 1)
        meta = jnp.zeros((owners, LANES), f32)
        for ids, count, base in ((listed, CAP, 0), (wanted, RCAP, CAP)):
            size = ids.shape[1]
            below = ids < bottom
            inside = jnp.logical_not(below) & (ids < bottom + rows_dev)
            start = jnp.sum(below.astype(f32), axis=1, keepdims=True).astype(jnp.int32)
            at = lax.broadcasted_iota(jnp.int32, (owners, size), 1) - start
            local = (ids - bottom - rows_dev).astype(f32)
            for k in range(count):
                value = jnp.sum(
                    jnp.where(inside & (at == k), local, 0.0), axis=1, keepdims=True
                )
                meta = jnp.where(lane == base + k, value + float(rows_dev), meta)
        payload[...] = blocks
        payload[pl.ds(CAP, owners, stride=SLOT), :] = meta


def picked(mask, value):
    high, low = split(value)
    rest = (value - high.astype(f32) - low.astype(f32)).astype(bf16)
    mask = mask.astype(bf16)
    return mm(
        jnp.concatenate([mask, mask, mask], axis=1),
        jnp.concatenate([high, low, rest], axis=0),
    )


def numbers(meta, owners, count, base):
    size = owners * count
    col = jnp.concatenate([meta[:, base + k : base + k + 1] for k in range(count)], axis=0)
    down = lax.broadcasted_iota(jnp.int32, (size, size), 0)
    along = lax.broadcasted_iota(jnp.int32, (size, size), 1)
    line = jnp.sum(jnp.where(down == along, col, 0.0), axis=0, keepdims=True)
    same = col == line
    earlier = jnp.sum(jnp.where(same & (down < along), 1.0, 0.0), axis=0, keepdims=True)
    return col, line, same, earlier == 0.0


def update_kernel(recv, table, accum, answers, new, place, metas, ids, old, found, sem):
    owners = recv.shape[0] // SLOT
    rows = table.shape[0]
    count = owners * CAP
    meta = recv[pl.ds(CAP, owners, stride=SLOT), :]
    metas[...] = meta.astype(jnp.int32)
    copy = pltpu.make_async_copy(metas, ids, sem)
    copy.start()
    grads = jnp.concatenate(
        [recv[pl.ds(k, owners, stride=SLOT), :] for k in range(CAP)], axis=0
    )
    col, line, same, once = numbers(meta, owners, CAP, 0)
    total = picked(same, grads)
    square = jnp.mean(total * total, axis=1, keepdims=True)
    valid = once & (line < float(rows))
    asks = jnp.concatenate([meta[:, CAP + k : CAP + k + 1] for k in range(RCAP)], axis=0)
    match = (asks == line) & valid
    lane = lax.broadcasted_iota(jnp.int32, (count, LANES), 1)
    number = col.astype(jnp.int32)
    mine = lane == number % LANES
    in_line = lax.broadcasted_iota(jnp.int32, (count, accum.shape[0]), 1) == number // LANES
    before = jnp.sum(jnp.where(mine, picked(in_line, accum[...]), 0.0), axis=1, keepdims=True)
    scale = RATE / (jnp.sqrt(before + square) + EPS)
    place[...] = jnp.where(mine, square, 0.0)
    hit = jnp.max(match.astype(f32), axis=1, keepdims=True) > 0.0
    copy.wait()

    def take(o, carry):
        for k in range(CAP):
            r = jnp.minimum(ids[o, k], rows - 1)
            old[pl.ds(k * owners + o, 1), :] = table[pl.ds(r, 1), :]
        for k in range(RCAP):
            r = jnp.minimum(ids[o, CAP + k], rows - 1)
            found[pl.ds(k * owners + o, 1), :] = table[pl.ds(r, 1), :]
        return carry

    lax.fori_loop(0, owners, take, 0, unroll=min(owners, 32))
    after = old[...] - total * scale
    new[...] = after
    out = jnp.where(hit, picked(match, after), found[...])
    for k in range(RCAP):
        answers[pl.ds(k, owners, stride=RCAP), :] = out[k * owners : (k + 1) * owners]


def store_kernel(recv, table, accum, new, place, new_table, new_accum, metas, ids, sem):
    owners = recv.shape[0] // SLOT
    rows = table.shape[0]
    count = owners * CAP
    meta = recv[pl.ds(CAP, owners, stride=SLOT), :]
    metas[...] = meta.astype(jnp.int32)
    copy = pltpu.make_async_copy(metas, ids, sem)
    copy.start()
    new_table[...] = table[...]
    _, line, _, once = numbers(meta, owners, CAP, 0)
    lines = accum.shape[0]
    row_hot = (
        lax.broadcasted_iota(jnp.int32, (lines, count), 0) == line.astype(jnp.int32) // LANES
    ) & (once & (line < float(rows)))
    new_accum[...] = accum[...] + picked(row_hot, place[...])
    copy.wait()

    def put(o, carry):
        for k in range(CAP):
            r = ids[o, k]

            @pl.when(r < rows)
            def _():
                new_table[pl.ds(r, 1), :] = new[pl.ds(k * owners + o, 1), :]

        return carry

    lax.fori_loop(0, owners, put, 0)


def gradients(
    owners,
    rows_dev,
    embeddings,
    cot_first,
    cot_second,
    cot_third,
    w_first,
    w_second,
    w_third,
    unique_ids,
    inverse,
    next_ids,
):
    samples, fields, embed = embeddings.shape
    maps = w_first.shape[0]
    fp = up(fields + 1, SUB)
    hp = up(maps, SUB)
    pairs = fp // 2
    fb = fp // SUB
    width = BLOCK * embed
    steps = samples // BLOCK

    emb_t = jnp.transpose(embeddings, (1, 0, 2))
    w1 = jnp.transpose(w_first, (1, 2, 0))
    w2 = jnp.transpose(w_second, (0, 2, 1))
    w3 = jnp.transpose(w_third, (0, 2, 1))

    arrays = (
        emb_t, cot_first, cot_second, cot_third, w1, w2, w3, unique_ids, next_ids, inverse
    )
    p1_rows = sum(4 * PACK * (fb - b) for b in range(fb))
    p2_rows = up(fields * hp, PACK)
    vmem = pl.BlockSpec(memory_space=pltpu.VMEM)
    return pl.pallas_call(
        functools.partial(grad_kernel, fields, rows_dev),
        grid=(steps,),
        out_shape=jax.ShapeDtypeStruct((owners * SLOT, embed), f32),
        in_specs=[pl.BlockSpec(memory_space=pl.ANY)] * 10,
        out_specs=vmem,
        scratch_shapes=[pltpu.VMEM(a.shape, a.dtype) for a in arrays]
        + [
            pltpu.SemaphoreType.DMA((len(arrays),)),
            pltpu.VMEM((fp * samples, LANES), f32),
            pltpu.VMEM((fp * samples, LANES), f32),
            pltpu.VMEM((samples, LANES), bf16),
            pltpu.VMEM((samples, LANES), bf16),
            pltpu.VMEM((fp * fp, LANES), f32),
            pltpu.VMEM((hp * fp, LANES), f32),
            pltpu.VMEM((hp * fp, LANES), f32),
            pltpu.VMEM((up(p1_rows, LANES), LANES), bf16),
            pltpu.VMEM((hp, up(p1_rows, LANES)), bf16),
            pltpu.VMEM((up(p2_rows, LANES), LANES), bf16),
            pltpu.VMEM((hp, up(p2_rows, LANES)), bf16),
            pltpu.VMEM((fp, width), f32),
            pltpu.VMEM((pairs, PACK, width), bf16),
            pltpu.VMEM((hp // SUB, PACK, width), bf16),
            pltpu.VMEM((p1_rows, width), bf16),
            pltpu.VMEM((p2_rows, width), bf16),
            pltpu.VMEM((hp, width), f32),
            pltpu.VMEM((LANES, width), bf16),
            pltpu.VMEM((LANES, width), bf16),
            pltpu.VMEM((LANES, width), bf16),
            pltpu.VMEM((hp, width), f32),
            pltpu.VMEM((BLOCK * fp * SUB, LANES), f32),
            pltpu.VMEM((fp, width), f32),
            pltpu.VMEM((samples * fp, LANES), f32),
        ],
        compiler_params=pltpu.CompilerParams(vmem_limit_bytes=56 * 2**20),
        name="gradients",
    )(*arrays)


def update(owners, recv, table, accum):
    embed = table.shape[1]
    vmem = pl.BlockSpec(memory_space=pltpu.VMEM)
    return pl.pallas_call(
        update_kernel,
        out_shape=(
            jax.ShapeDtypeStruct((owners * RCAP, embed), f32),
            jax.ShapeDtypeStruct((owners * CAP, embed), f32),
            jax.ShapeDtypeStruct((owners * CAP, embed), f32),
        ),
        in_specs=[vmem] * 3,
        out_specs=(vmem,) * 3,
        scratch_shapes=[
            pltpu.VMEM((owners, LANES), jnp.int32),
            pltpu.SMEM((owners, LANES), jnp.int32),
            pltpu.VMEM((owners * CAP, LANES), f32),
            pltpu.VMEM((owners * RCAP, LANES), f32),
            pltpu.SemaphoreType.DMA,
        ],
        compiler_params=pltpu.CompilerParams(vmem_limit_bytes=48 * 2**20),
        name="update",
    )(recv, table, accum)


def local(
    embeddings,
    cot_first,
    cot_second,
    cot_third,
    w_first,
    w_second,
    w_third,
    unique_ids,
    inverse,
    table,
    accum,
    next_ids,
):
    owners = lax.axis_size("group") * lax.axis_size("member")
    rows_dev, embed = table.shape
    vmem = pl.BlockSpec(memory_space=pltpu.VMEM)
    payload = gradients(
        owners,
        rows_dev,
        embeddings,
        cot_first,
        cot_second,
        cot_third,
        w_first,
        w_second,
        w_third,
        unique_ids,
        inverse,
        next_ids,
    )
    axes = ("group", "member")
    recv = lax.all_to_all(payload, axes, split_axis=0, concat_axis=0, tiled=True)
    lines = rows_dev // LANES
    accum = accum.reshape(lines, LANES)
    answers, new, place = update(owners, recv, table, accum)
    back = lax.all_to_all(answers, axes, split_axis=0, concat_axis=0, tiled=True)
    new_table, new_accum = pl.pallas_call(
        store_kernel,
        out_shape=(
            jax.ShapeDtypeStruct((rows_dev, embed), f32),
            jax.ShapeDtypeStruct((lines, LANES), f32),
        ),
        in_specs=[vmem] * 5,
        out_specs=(vmem,) * 2,
        scratch_shapes=[
            pltpu.VMEM((owners, LANES), jnp.int32),
            pltpu.SMEM((owners, LANES), jnp.int32),
            pltpu.SemaphoreType.DMA,
        ],
        compiler_params=pltpu.CompilerParams(vmem_limit_bytes=48 * 2**20),
        cost_estimate=pl.CostEstimate(
            flops=2 * lines * 3 * owners * CAP * LANES,
            bytes_accessed=2 * rows_dev * embed * 4,
            transcendentals=0,
        ),
        name="store",
    )(recv, table, accum, new, place)

    wanted = next_ids[0]
    owner_of = wanted // rows_dev
    leading = jnp.sum((owner_of[None, :] < owner_of[:, None]).astype(jnp.int32), axis=1)
    within = jnp.arange(wanted.shape[0], dtype=jnp.int32) - leading
    returned = back[owner_of * RCAP + within]
    return (new_table, new_accum.reshape(rows_dev), returned[None])


def solution(mesh):
    both = ("group", "member")
    in_specs = (
        P(both, None, None),
        P(both, None),
        P(both, None),
        P(both, None),
        P(),
        P(),
        P(),
        P(both, None),
        P(both, None),
        P(both, None),
        P(both),
        P(both, None),
    )
    out_specs = (P(both, None), P(both), P(both, None, None))
    return jax.shard_map(local, mesh=mesh, in_specs=in_specs, out_specs=out_specs, check_vma=False)
```

```python
import functools

import jax
import jax.numpy as jnp
from jax import lax
from jax.experimental import pallas as pl
from jax.experimental.pallas import tpu as pltpu
from jax.sharding import PartitionSpec as P

CAP = 4
RCAP = 8

RATE = 0.5
EPS = 1e-08

LANES = 128
SUB = 8
PACK = 16
SLOT = 8
TILE = 256
BLOCK = 16

f32 = jnp.float32
bf16 = jnp.bfloat16


def up(value, unit):
    return -(-value // unit) * unit


def split(value):
    high = value.astype(bf16)
    return high, (value - high.astype(f32)).astype(bf16)


def mm(a, b):
    return jnp.dot(a, b, preferred_element_type=f32)


def mm_t(a, b):
    return lax.dot_general(a, b, (((0,), (0,)), ((), ())), preferred_element_type=f32)


def grad_kernel(
    fields,
    rows_dev,
    emb_in,
    c1_in,
    c2_in,
    c3_in,
    w1_in,
    w2_in,
    w3_in,
    uid_in,
    nid_in,
    inv_in,
    payload,
    emb,
    c1,
    c2,
    c3,
    w1,
    w2,
    w3,
    uid,
    nid,
    inv,
    sems,
    xs,
    top,
    c1s,
    c3s,
    w1f,
    w2f,
    w3f,
    w1s,
    w1t,
    w2s,
    w2t,
    xf,
    xp,
    dy,
    p1,
    p2,
    y1s,
    y2s,
    us,
    ls,
    acc,
    part,
    grad,
    gs,
):
    step = pl.program_id(0)
    samples = inv.shape[0]
    maps = c1.shape[1]
    fp = xf.shape[0]
    hp = acc.shape[0]
    hb = hp // SUB
    fb = fp // SUB
    pairs = fp // 2
    full = fields // 2
    width = xf.shape[1]

    def stacked(j, b):
        if j < 2 * full:
            return (j // 2) * 2 * hp + b * PACK + (j % 2) * SUB
        return full * 2 * hp + b * SUB

    def offsets():
        place = 0
        for m in range(pairs):
            ib = (2 * m) // SUB
            for jb in range(ib, fb):
                yield m, ib, jb, place
                place += PACK

    sources = (emb_in, c1_in, c2_in, c3_in, w1_in, w2_in, w3_in, uid_in, nid_in, inv_in)
    targets = (emb, c1, c2, c3, w1, w2, w3, uid, nid, inv)

    def fetch(q):
        return pltpu.make_async_copy(sources[q], targets[q], sems.at[q])

    @pl.when(step == 0)
    def _():
        for q in (0, 4, 3, 2, 1, 6, 5, 9, 7, 8):
            fetch(q).start()
        us[...] = jnp.zeros_like(us)
        ls[...] = jnp.zeros_like(ls)
        y2s[...] = jnp.zeros_like(y2s)
        part[...] = jnp.zeros_like(part)
        w1s[...] = jnp.zeros_like(w1s)
        w1f[...] = jnp.zeros_like(w1f)
        w2f[...] = jnp.zeros_like(w2f)
        w3f[...] = jnp.zeros_like(w3f)
        c1s[...] = jnp.zeros_like(c1s)
        c3s[...] = jnp.zeros_like(c3s)
        fetch(0).wait()
        xs[pl.ds(0, fields * samples), :] = (
            emb[...].astype(f32).reshape(fields * samples, LANES)
        )
        xs[pl.ds(fields * samples, samples), :] = jnp.zeros((samples, LANES), f32)
        fetch(4).wait()
        for i in range(fields):
            w1f[pl.ds(i * fp, fields), 0:maps] = w1[i].astype(f32)
        for m, ib, jb, place in offsets():
            two = []
            for s in range(2):
                i = 2 * m + s
                direct = w1f[pl.ds(i * fp + SUB * jb, SUB), :]
                two.append(direct + w1f[pl.ds(SUB * jb * fp + i, SUB, stride=fp), :])
            w1s[pl.ds(place, PACK), :] = jnp.concatenate(two, axis=0).astype(bf16)
        for c in range(w1s.shape[0] // LANES):
            w1t[:, c * LANES : (c + 1) * LANES] = (
                w1s[c * LANES : (c + 1) * LANES, :].astype(f32).T[0:hp].astype(bf16)
            )
        fetch(6).wait()
        for h in range(maps):
            w3f[pl.ds(h * fp, fields), 0:maps] = w3[h].astype(f32)
        fetch(3).wait()
        c3s[:, 0:maps] = c3[...]
        for j in range(fields):
            top[pl.ds(j * samples, samples), :] = mm(
                c3s[:, 0:hp], w3f[pl.ds(j, hp, stride=fp), :].astype(bf16)
            )
        top[pl.ds(fields * samples, samples), :] = jnp.zeros((samples, LANES), f32)
        fetch(2).wait()
        top[pl.ds(fields * samples, samples), 0:maps] = c2[...].astype(f32)
        fetch(1).wait()
        c1s[:, 0:maps] = c1[...]
        fetch(5).wait()
        for h in range(maps):
            w2f[pl.ds(h * fp, fields), 0:maps] = w2[h].astype(f32)
        zeros = jnp.zeros((LANES - hp, LANES), f32)
        for m in range(full):
            two = []
            for s in range(2):
                flat = w2f[pl.ds(2 * m + s, hp, stride=fp), :]
                flat = jnp.concatenate([flat, zeros], axis=0)
                two.append(flat.T[0:hp].reshape(hb, SUB, LANES))
            w2s[pl.ds(m * 2 * hp, 2 * hp), :] = (
                jnp.stack(two, axis=1).reshape(2 * hp, LANES).astype(bf16)
            )
        rest = jnp.zeros((w2s.shape[0] - full * 2 * hp, LANES), f32)
        if fields % 2:
            flat = w2f[pl.ds(fields - 1, hp, stride=fp), :]
            flat = jnp.concatenate([flat, zeros], axis=0)
            rest = jnp.concatenate([flat.T[0:hp], rest[hp:]], axis=0)
        w2s[pl.ds(full * 2 * hp, rest.shape[0]), :] = rest.astype(bf16)
        for c in range(w2s.shape[0] // LANES):
            w2t[:, c * LANES : (c + 1) * LANES] = (
                w2s[c * LANES : (c + 1) * LANES, :].astype(f32).T[0:hp].astype(bf16)
            )
        fetch(9).wait()
        fetch(7).wait()
        fetch(8).wait()

    first = step * BLOCK
    for k in range(BLOCK):
        xf[:, k * LANES : (k + 1) * LANES] = xs[pl.ds(first + k, fp, stride=samples), :]
    for m in range(pairs):
        xp[m] = jnp.concatenate(
            [jnp.broadcast_to(xf[2 * m + s : 2 * m + s + 1, :], (SUB, width)) for s in range(2)],
            axis=0,
        ).astype(bf16)
    twice = []
    for b in range(fb):
        block = xf[SUB * b : SUB * (b + 1), :]
        twice.append(jnp.concatenate([block, block], axis=0).astype(bf16))
    half = [t * jnp.asarray(0.5, bf16) for t in twice]
    for m, ib, jb, place in offsets():
        p1[pl.ds(place, PACK), :] = xp[m] * (half[jb] if jb == ib else twice[jb])
    layer_one = mm(w1t[:, 0 : p1.shape[0]], p1[...]).astype(bf16).astype(f32)
    y1s[...] = layer_one
    for b in range(hb):
        block = y1s[SUB * b : SUB * (b + 1), :]
        dy[b] = jnp.concatenate([block, block], axis=0).astype(bf16)
    for m in range(full):
        for b in range(hb):
            p2[pl.ds(m * 2 * hp + b * PACK, PACK), :] = xp[m] * dy[b]
    if fields % 2:
        alone = jnp.broadcast_to(xf[fields - 1 : fields, :], (PACK, width)).astype(bf16)
        for b in range(0, hb, 2):
            block = y1s[SUB * b : SUB * min(b + 2, hb), :]
            if b + 1 == hb:
                block = jnp.concatenate([block, jnp.zeros_like(block)], axis=0)
            p2[pl.ds(full * 2 * hp + b * SUB, PACK), :] = alone * block.astype(bf16)
    y2s[0:hp, :] = mm(w2t[:, 0 : p2.shape[0]], p2[...]).astype(bf16)

    last_row = lax.broadcasted_iota(jnp.int32, (fp, LANES), 0) == fields
    for k in range(BLOCK):
        here = slice(k * LANES, (k + 1) * LANES)
        high, low = split(top[pl.ds(first + k, fp, stride=samples), :])
        own = jnp.where(last_row, 1.0, xf[:, here]).astype(bf16)
        us[:, here] = mm_t(
            jnp.concatenate([high, low], axis=0), jnp.concatenate([own, own], axis=0)
        ).astype(bf16)
        y2 = y2s[:, here]
        gs[pl.ds((first + k) * fp, fp), :] = mm(
            jnp.concatenate([high, low], axis=1), jnp.concatenate([y2, y2], axis=0)
        )

    pick = (
        lax.broadcasted_iota(jnp.int32, (samples, width), 0)
        == first + lax.broadcasted_iota(jnp.int32, (samples, width), 1) // LANES
    )
    acc[...] = mm_t(c1s[...], pick.astype(bf16))[0:hp]
    group = 20
    for cut in range(0, width, TILE):
        cols = slice(cut, cut + TILE)
        samples_here = range(cut // LANES, (cut + TILE) // LANES)
        for j0 in range(0, fields, 2 * group):
            js = range(j0, min(j0 + 2 * group, fields))
            base = stacked(j0, 0)
            z = mm(w2s[base : stacked(js[-1], hb - 1) + SUB, :], us[:, cols])
            factors = [xf[j : j + 1, cols] for j in js]
            sums = [None] * len(js)
            for b in range(hb):
                rows = slice(SUB * b, SUB * (b + 1))
                one = y1s[rows, cols]
                total = acc[rows, cols]
                for q, j in enumerate(js):
                    at = stacked(j, b) - base
                    zj = z[at : at + SUB]
                    total = total + zj * factors[q]
                    term = zj * one
                    sums[q] = term if sums[q] is None else sums[q] + term
                acc[rows, cols] = total
            for q, j in enumerate(js):
                for k in samples_here:
                    part[pl.ds((k * fp + j) * SUB, SUB), :] = sums[q][
                        :, k * LANES - cut : (k + 1) * LANES - cut
                    ]
    ls[0:hp, :] = acc[...].astype(bf16)

    for cut in range(0, width, TILE):
        cols = slice(cut, cut + TILE)
        samples_here = range(cut // LANES, (cut + TILE) // LANES)
        z = mm(w1s[0 : p1.shape[0], :], ls[:, cols])
        totals = [None] * fb
        for m in range(pairs):
            ib = (2 * m) // SUB
            place = [q for q in offsets() if q[0] == m]
            for s in range(2):
                i = 2 * m + s
                if i >= fields:
                    continue
                factor = xf[i : i + 1, cols]
                across = None
                for _, _, jb, at in place:
                    zj = z[at + SUB * s : at + SUB * (s + 1)]
                    term = zj * factor
                    totals[jb] = term if totals[jb] is None else totals[jb] + term
                    if jb > ib:
                        term = zj * xf[SUB * jb : SUB * (jb + 1), cols]
                        across = term if across is None else across + term
                if across is not None:
                    for k in samples_here:
                        part[pl.ds((k * fp + i) * SUB, SUB), :] += across[
                            :, k * LANES - cut : (k + 1) * LANES - cut
                        ]
        for jb in range(fb):
            grad[SUB * jb : SUB * (jb + 1), cols] = totals[jb]

    for k in range(BLOCK):
        here = slice(k * LANES, (k + 1) * LANES)
        mine = grad[:, here]
        for s in range(SUB):
            mine = mine + part[pl.ds(k * fp * SUB + s, fp, stride=SUB), :]
        gs[pl.ds((first + k) * fp, fp), :] += mine

    @pl.when(step == pl.num_programs(0) - 1)
    def _():
        owners = payload.shape[0] // SLOT
        rows = owners * SLOT
        positions = uid.shape[1]
        named = []
        for n in range(samples):
            named.append(inv[n : n + 1, :])
            named.append(jnp.full((1, fp - fields), -1, jnp.int32))
        named = jnp.concatenate(named, axis=1)
        chosen = (
            lax.broadcasted_iota(jnp.int32, (positions, samples * fp), 0)
            == jnp.broadcast_to(named, (positions, samples * fp))
        ).astype(bf16)
        high, low = split(gs[...])
        merged = mm(chosen, high) + mm(chosen, low)

        listed = uid[...]
        wanted = nid[...]
        row = lax.broadcasted_iota(jnp.int32, (rows, 1), 0)
        owner = row // SLOT
        slot = row % SLOT
        bottom = owner * rows_dev
        start = jnp.sum((listed < bottom).astype(f32), axis=1, keepdims=True).astype(jnp.int32)
        at = lax.broadcasted_iota(jnp.int32, (rows, positions), 1)
        inside = (listed >= bottom) & (listed < bottom + rows_dev)
        chosen = ((at == start + slot) & inside & (slot < CAP)).astype(bf16)
        high, low = split(merged)
        blocks = mm(chosen, high) + mm(chosen, low)
        owner = lax.broadcasted_iota(jnp.int32, (owners, 1), 0)
        bottom = owner * rows_dev
        lane = lax.broadcasted_iota(jnp.int32, (owners, LANES), 1)
        meta = jnp.zeros((owners, LANES), f32)
        for ids, count, base in ((listed, CAP, 0), (wanted, RCAP, CAP)):
            size = ids.shape[1]
            below = ids < bottom
            inside = jnp.logical_not(below) & (ids < bottom + rows_dev)
            start = jnp.sum(below.astype(f32), axis=1, keepdims=True).astype(jnp.int32)
            at = lax.broadcasted_iota(jnp.int32, (owners, size), 1) - start
            local = (ids - bottom - rows_dev).astype(f32)
            for k in range(count):
                value = jnp.sum(
                    jnp.where(inside & (at == k), local, 0.0), axis=1, keepdims=True
                )
                meta = jnp.where(lane == base + k, value + float(rows_dev), meta)
        payload[...] = blocks
        payload[pl.ds(CAP, owners, stride=SLOT), :] = meta


def picked(mask, value):
    high, low = split(value)
    rest = (value - high.astype(f32) - low.astype(f32)).astype(bf16)
    mask = mask.astype(bf16)
    return mm(
        jnp.concatenate([mask, mask, mask], axis=1),
        jnp.concatenate([high, low, rest], axis=0),
    )


def numbers(meta, owners, count, base):
    size = owners * count
    col = jnp.concatenate([meta[:, base + k : base + k + 1] for k in range(count)], axis=0)
    down = lax.broadcasted_iota(jnp.int32, (size, size), 0)
    along = lax.broadcasted_iota(jnp.int32, (size, size), 1)
    line = jnp.sum(jnp.where(down == along, col, 0.0), axis=0, keepdims=True)
    same = col == line
    earlier = jnp.sum(jnp.where(same & (down < along), 1.0, 0.0), axis=0, keepdims=True)
    return col, line, same, earlier == 0.0


def update_kernel(recv, table, accum, answers, new, place, metas, ids, old, found, sem):
    owners = recv.shape[0] // SLOT
    rows = table.shape[0]
    count = owners * CAP
    meta = recv[pl.ds(CAP, owners, stride=SLOT), :]
    metas[...] = meta.astype(jnp.int32)
    copy = pltpu.make_async_copy(metas, ids, sem)
    copy.start()
    grads = jnp.concatenate(
        [recv[pl.ds(k, owners, stride=SLOT), :] for k in range(CAP)], axis=0
    )
    col, line, same, once = numbers(meta, owners, CAP, 0)
    total = picked(same, grads)
    square = jnp.mean(total * total, axis=1, keepdims=True)
    valid = once & (line < float(rows))
    asks = jnp.concatenate([meta[:, CAP + k : CAP + k + 1] for k in range(RCAP)], axis=0)
    match = (asks == line) & valid
    lane = lax.broadcasted_iota(jnp.int32, (count, LANES), 1)
    number = col.astype(jnp.int32)
    mine = lane == number % LANES
    in_line = lax.broadcasted_iota(jnp.int32, (count, accum.shape[0]), 1) == number // LANES
    before = jnp.sum(jnp.where(mine, picked(in_line, accum[...]), 0.0), axis=1, keepdims=True)
    scale = RATE / (jnp.sqrt(before + square) + EPS)
    place[...] = jnp.where(mine, square, 0.0)
    hit = jnp.max(match.astype(f32), axis=1, keepdims=True) > 0.0
    copy.wait()

    def take(o, carry):
        for k in range(CAP):
            r = jnp.minimum(ids[o, k], rows - 1)
            old[pl.ds(k * owners + o, 1), :] = table[pl.ds(r, 1), :]
        for k in range(RCAP):
            r = jnp.minimum(ids[o, CAP + k], rows - 1)
            found[pl.ds(k * owners + o, 1), :] = table[pl.ds(r, 1), :]
        return carry

    lax.fori_loop(0, owners, take, 0, unroll=min(owners, 32))
    after = old[...] - total * scale
    new[...] = after
    out = jnp.where(hit, picked(match, after), found[...])
    for k in range(RCAP):
        answers[pl.ds(k, owners, stride=RCAP), :] = out[k * owners : (k + 1) * owners]


def store_kernel(recv, table, accum, new, place, new_table, new_accum, metas, ids, sem):
    owners = recv.shape[0] // SLOT
    rows = table.shape[0]
    count = owners * CAP
    meta = recv[pl.ds(CAP, owners, stride=SLOT), :]
    metas[...] = meta.astype(jnp.int32)
    copy = pltpu.make_async_copy(metas, ids, sem)
    copy.start()
    new_table[...] = table[...]
    _, line, _, once = numbers(meta, owners, CAP, 0)
    lines = accum.shape[0]
    row_hot = (
        lax.broadcasted_iota(jnp.int32, (lines, count), 0) == line.astype(jnp.int32) // LANES
    ) & (once & (line < float(rows)))
    new_accum[...] = accum[...] + picked(row_hot, place[...])
    copy.wait()

    def put(o, carry):
        for k in range(CAP):
            r = ids[o, k]

            @pl.when(r < rows)
            def _():
                new_table[pl.ds(r, 1), :] = new[pl.ds(k * owners + o, 1), :]

        return carry

    lax.fori_loop(0, owners, put, 0)


def gradients(
    owners,
    rows_dev,
    embeddings,
    cot_first,
    cot_second,
    cot_third,
    w_first,
    w_second,
    w_third,
    unique_ids,
    inverse,
    next_ids,
):
    samples, fields, embed = embeddings.shape
    maps = w_first.shape[0]
    fp = up(fields + 1, SUB)
    hp = up(maps, SUB)
    pairs = fp // 2
    fb = fp // SUB
    width = BLOCK * embed
    steps = samples // BLOCK

    emb_t = jnp.transpose(embeddings, (1, 0, 2))
    w1 = jnp.transpose(w_first, (1, 2, 0))
    w2 = jnp.transpose(w_second, (0, 2, 1))
    w3 = jnp.transpose(w_third, (0, 2, 1))

    arrays = (
        emb_t, cot_first, cot_second, cot_third, w1, w2, w3, unique_ids, next_ids, inverse
    )
    p1_rows = sum(4 * PACK * (fb - b) for b in range(fb))
    p2_rows = up(fields * hp, PACK)
    vmem = pl.BlockSpec(memory_space=pltpu.VMEM)
    return pl.pallas_call(
        functools.partial(grad_kernel, fields, rows_dev),
        grid=(steps,),
        out_shape=jax.ShapeDtypeStruct((owners * SLOT, embed), f32),
        in_specs=[pl.BlockSpec(memory_space=pl.ANY)] * 10,
        out_specs=vmem,
        scratch_shapes=[pltpu.VMEM(a.shape, a.dtype) for a in arrays]
        + [
            pltpu.SemaphoreType.DMA((len(arrays),)),
            pltpu.VMEM(((fp + 1) * samples, LANES), f32),
            pltpu.VMEM(((fp + 1) * samples, LANES), f32),
            pltpu.VMEM((samples, LANES), bf16),
            pltpu.VMEM((samples, LANES), bf16),
            pltpu.VMEM((fp * fp, LANES), f32),
            pltpu.VMEM((hp * fp, LANES), f32),
            pltpu.VMEM((hp * fp, LANES), f32),
            pltpu.VMEM((up(p1_rows, LANES), LANES), bf16),
            pltpu.VMEM((hp, up(p1_rows, LANES)), bf16),
            pltpu.VMEM((up(p2_rows, LANES), LANES), bf16),
            pltpu.VMEM((hp, up(p2_rows, LANES)), bf16),
            pltpu.VMEM((fp, width), f32),
            pltpu.VMEM((pairs, PACK, width), bf16),
            pltpu.VMEM((hp // SUB, PACK, width), bf16),
            pltpu.VMEM((p1_rows, width), bf16),
            pltpu.VMEM((p2_rows, width), bf16),
            pltpu.VMEM((hp, width), f32),
            pltpu.VMEM((LANES, width), bf16),
            pltpu.VMEM((LANES, width), bf16),
            pltpu.VMEM((LANES, width), bf16),
            pltpu.VMEM((hp, width), f32),
            pltpu.VMEM((BLOCK * fp * SUB, LANES), f32),
            pltpu.VMEM((fp, width), f32),
            pltpu.VMEM((samples * fp, LANES), f32),
        ],
        compiler_params=pltpu.CompilerParams(vmem_limit_bytes=56 * 2**20),
        name="gradients",
    )(*arrays)


def update(owners, recv, table, accum):
    embed = table.shape[1]
    vmem = pl.BlockSpec(memory_space=pltpu.VMEM)
    return pl.pallas_call(
        update_kernel,
        out_shape=(
            jax.ShapeDtypeStruct((owners * RCAP, embed), f32),
            jax.ShapeDtypeStruct((owners * CAP, embed), f32),
            jax.ShapeDtypeStruct((owners * CAP, embed), f32),
        ),
        in_specs=[vmem] * 3,
        out_specs=(vmem,) * 3,
        scratch_shapes=[
            pltpu.VMEM((owners, LANES), jnp.int32),
            pltpu.SMEM((owners, LANES), jnp.int32),
            pltpu.VMEM((owners * CAP, LANES), f32),
            pltpu.VMEM((owners * RCAP, LANES), f32),
            pltpu.SemaphoreType.DMA,
        ],
        compiler_params=pltpu.CompilerParams(vmem_limit_bytes=48 * 2**20),
        name="update",
    )(recv, table, accum)


def local(
    embeddings,
    cot_first,
    cot_second,
    cot_third,
    w_first,
    w_second,
    w_third,
    unique_ids,
    inverse,
    table,
    accum,
    next_ids,
):
    owners = lax.axis_size("group") * lax.axis_size("member")
    rows_dev, embed = table.shape
    vmem = pl.BlockSpec(memory_space=pltpu.VMEM)
    payload = gradients(
        owners,
        rows_dev,
        embeddings,
        cot_first,
        cot_second,
        cot_third,
        w_first,
        w_second,
        w_third,
        unique_ids,
        inverse,
        next_ids,
    )
    axes = ("group", "member")
    recv = lax.all_to_all(payload, axes, split_axis=0, concat_axis=0, tiled=True)
    lines = rows_dev // LANES
    accum = accum.reshape(lines, LANES)
    answers, new, place = update(owners, recv, table, accum)
    back = lax.all_to_all(answers, axes, split_axis=0, concat_axis=0, tiled=True)
    new_table, new_accum = pl.pallas_call(
        store_kernel,
        out_shape=(
            jax.ShapeDtypeStruct((rows_dev, embed), f32),
            jax.ShapeDtypeStruct((lines, LANES), f32),
        ),
        in_specs=[vmem] * 5,
        out_specs=(vmem,) * 2,
        scratch_shapes=[
            pltpu.VMEM((owners, LANES), jnp.int32),
            pltpu.SMEM((owners, LANES), jnp.int32),
            pltpu.SemaphoreType.DMA,
        ],
        compiler_params=pltpu.CompilerParams(vmem_limit_bytes=48 * 2**20),
        cost_estimate=pl.CostEstimate(
            flops=2 * lines * 3 * owners * CAP * LANES,
            bytes_accessed=2 * rows_dev * embed * 4,
            transcendentals=0,
        ),
        name="store",
    )(recv, table, accum, new, place)

    wanted = next_ids[0]
    owner_of = wanted // rows_dev
    leading = jnp.sum((owner_of[None, :] < owner_of[:, None]).astype(jnp.int32), axis=1)
    within = jnp.arange(wanted.shape[0], dtype=jnp.int32) - leading
    returned = back[owner_of * RCAP + within]
    return (new_table, new_accum.reshape(rows_dev), returned[None])


def solution(mesh):
    both = ("group", "member")
    in_specs = (
        P(both, None, None),
        P(both, None),
        P(both, None),
        P(both, None),
        P(),
        P(),
        P(),
        P(both, None),
        P(both, None),
        P(both, None),
        P(both),
        P(both, None),
    )
    out_specs = (P(both, None), P(both), P(both, None, None))
    return jax.shard_map(local, mesh=mesh, in_specs=in_specs, out_specs=out_specs, check_vma=False)
```
